32 devices in a mesh: mu: 8 (over z, y), pa: 4 (over x, core).
Axes of the slice: x: 2, y: 2, z: 4, core: 2. Of those that a mesh axis runs over, the one named last changes fastest.
Arguments:
- three_center: bfloat16 [40, 64, 16384], P('mu', None, 'pa'), may hold values from -6 to 6
- pair_mu: int32 [8, 5], P('mu'), may hold values from 0 to 47
- pair_site: int32 [8, 5, 1], P('mu'), may hold values from 0 to 3; in each aligned block of 5 rows (0 to 4, 5 to 9, ..., all dimensions but the last counted through in order) at most 2 rows name the same one
- pair_pos: int32 [8, 5], P('mu'), may hold values from 0 to 11
- coeff: bfloat16 [3072, 2], replicated, may hold values from -0.21875 to 0.21875
- fitting: bfloat16 [48, 256, 256], P(None, 'pa'), as said below
Outputs:
- gfit: bfloat16 [8, 12, 1, 16384], P('mu', None, None, 'pa')
The draws below stay inside these ranges and needn't reach their ends.
Inputs may be any that keep to these rules, and one draw needn't show every extreme that they name: `pair_site`: of the 5 pairs listed for one index of mu, at most 2 name the same site, and 2 is reached. Every fitting[b] is a symmetric matrix.
All inputs are finite; a program needn't handle non-finite values.
Results may differ from the reference program's by a relative error of at most 0.0058.
Values may be sent and summed in bfloat16 or wider, within the bound.
A program may use at most 64 MiB of HBM per device.

```python
import math
import jax
import jax.numpy as jnp
import numpy as np
from jax import lax

BS = 64
PL = 256
PLS = 64
SITES = 4
NU_SITE = 12
NBO = 48
NAO = 3072
NT = 5
CAP = 2
IG_SZ = 1
NOB = 2
N_MU = 8
N_PA = 4


def draw_fitting(key, part):
    shape = (NBO, PL, PL)
    base = jax.random.normal(key, shape, jnp.float32)
    symmetric = (base + jnp.swapaxes(base, 1, 2)) * 0.5 ** 0.5 * PL ** (-0.5)
    return symmetric.astype(jnp.bfloat16)


def set_ends(drawn, key, least, largest):
    longest = drawn.shape.index(max(drawn.shape))
    spots = []
    for shift in (0, 1):
        where = [jax.random.randint(jax.random.fold_in(key, axis), (), 0, length) for axis, length in enumerate(drawn.shape)]
        where[longest] = (where[longest] + shift) % drawn.shape[longest]
        spots.append(tuple(where))
    return drawn.at[spots[0]].set(least).at[spots[1]].set(largest)


def steps_of(key, shape, pieces, low, top_value):
    level = 1.0
    for position, blocks in pieces:
        steps = jax.random.uniform(jax.random.fold_in(jax.random.fold_in(key, 6), position), (blocks,), jnp.float32, low / len(pieces), top_value / len(pieces))
        level = level * jnp.repeat(jnp.exp(steps), shape[position] // blocks).reshape((-1,) + (1,) * (len(shape) - 1 - position))
    return level


def routed_block(stream_key, own, number, rows, count, top, limit, slope):
    order = jax.random.permutation(stream_key, count)
    heavy_load, common = load_shares(count, rows * top, limit, slope, True), load_shares(count, rows * top, limit, slope, False)
    places = jnp.arange(count)

    def named(tallies, turn):
        used = int((tallies > 0).sum())
        fixed = max(1, used // 4)
        shifted = fixed + (places - fixed + turn * (used - fixed)) % max(1, count - fixed)
        return jnp.zeros((count,), jnp.int32).at[order[jnp.where(places < fixed, places, shifted)]].set(jnp.asarray(tallies, jnp.int32))

    tallies = jnp.where(number % 4 == 0, named(heavy_load, number // 4), named(common, number - number // 4 - 1))
    mixed = jax.random.permutation(jax.random.fold_in(own, 3), count)
    source_of, sink = mixed[0:count // 2 * 2:2], mixed[1:count // 2 * 2:2]
    slack = jnp.minimum(tallies[source_of] - 1, limit - tallies[sink]) // 2
    slack = jnp.where((source_of == order[0]) | (sink == order[0]) | (tallies[sink] == 0), 0, jnp.maximum(slack, 0))
    shifted = jax.random.randint(jax.random.fold_in(own, 4), (count // 2,), 0, 1 << 20) % (slack + 1)
    tallies = tallies.at[source_of].add(-shifted).at[sink].add(shifted)
    items = jnp.searchsorted(jnp.cumsum(tallies), jnp.arange(rows * top), side="right").astype(jnp.int32)
    table = items.reshape(top, rows).T
    table = table[jax.random.permutation(jax.random.fold_in(own, 1), rows)]
    turn = jax.random.randint(jax.random.fold_in(own, 2), (rows, 1), 0, top)
    return jnp.take_along_axis(table, (jnp.arange(top)[None, :] + turn) % top, axis=1)


def load_shares(count, total, reach, skew, full):
    loads = [(1 << 20) // math.isqrt(standing ** skew) + 1 for standing in range(1, count + 1)]
    largest = reach if full else min(reach, max(-(-total // count), total * loads[0] // sum(loads)))
    least = 1 if total - largest >= count - 1 else 0
    given, spare = [largest] + [least] * (count - 1), total - largest - least * (count - 1)
    while spare > 0:
        candidates = [i for i in range(1, count) if given[i] < largest] or [i for i in range(1, count) if given[i] < reach]
        whole, remaining = sum([loads[i] for i in candidates]), spare
        for i in candidates:
            extra = min(reach - given[i], max(1, remaining * loads[i] // whole), spare)
            given[i] = given[i] + extra
            spare = spare - extra
    return np.array(given)


def centred(rng, extent, width, most, shards=(), held_as=jnp.bfloat16):
    result = width * jax.random.normal(rng, extent, jnp.float32)
    if shards:
        result = result * steps_of(rng, extent, shards, -0.22, 0.18)
    return jnp.clip(result, -most, most).astype(held_as)


def setup_inputs(seed: int = 0) -> dict:
    arg_keys = jax.random.split(jax.random.key(seed), 7)
    three_center = centred(arg_keys[0], (N_MU * NT, BS, N_PA * BS * PLS), 1.0, 6.0, ((0, 8), (2, 4)))
    pair_mu = set_ends(jax.random.randint(arg_keys[1], (N_MU, NT), 0, NBO), jax.random.fold_in(arg_keys[1], 1), 0, NBO - 1).astype(jnp.int32)
    pair_site_keys = jax.random.split(jax.random.fold_in(arg_keys[2], 1), N_MU * NT // NT)
    pair_site_turns = jax.random.permutation(jax.random.fold_in(arg_keys[2], 3), N_MU * NT // NT)
    pair_site = jax.vmap(lambda own, number: routed_block(jax.random.fold_in(arg_keys[2], 2), own, number, NT, SITES, 1, CAP, 2))(pair_site_keys, pair_site_turns).reshape((N_MU, NT, 1))
    pair_pos = set_ends(jax.random.randint(arg_keys[3], (N_MU, NT), 0, NU_SITE), jax.random.fold_in(arg_keys[3], 1), 0, NU_SITE - 1).astype(jnp.int32)
    coeff = centred(arg_keys[4], (NAO, NOB), (BS * NU_SITE) ** -0.5, 0.21875)
    fitting = draw_fitting(jax.random.fold_in(arg_keys[6], 71), 0)
    return {"three_center": three_center, "pair_mu": pair_mu, "pair_site": pair_site, "pair_pos": pair_pos, "coeff": coeff, "fitting": fitting}


def reference(three_center, pair_mu, pair_site, pair_pos, coeff, fitting):
    groups = N_MU // SITES
    full_width = N_PA * BS * PLS
    mu_blocks = coeff.reshape(NBO, BS, NOB)
    mu_list = pair_mu.reshape(-1).astype(jnp.int32)
    site_list = pair_site.reshape(-1).astype(jnp.int32)
    pos_list = pair_pos.reshape(-1).astype(jnp.int32)

    def add_pair(fitted, pair_index):
        block_rows = lax.dynamic_index_in_dim(mu_blocks, mu_list[pair_index], 0, keepdims=False)
        slab_rows = lax.dynamic_index_in_dim(three_center, pair_index, 0, keepdims=False)
        piece_sum = jnp.dot(block_rows.T, slab_rows, preferred_element_type=jnp.float32).astype(jnp.bfloat16)
        piece_sum = lax.optimization_barrier(piece_sum).astype(jnp.float32).reshape(groups, IG_SZ, full_width)
        updated = fitted.at[:, site_list[pair_index], pos_list[pair_index]].add(piece_sum)
        return updated, None

    initial = jnp.zeros((groups, SITES, NU_SITE, IG_SZ, full_width), jnp.float32)
    fitted, unused_out = lax.scan(add_pair, initial, jnp.arange(N_MU * NT, dtype=jnp.int32))
    rounded = fitted.astype(jnp.bfloat16).reshape(N_MU, NU_SITE, IG_SZ, N_PA, BS, PLS)
    arranged = jnp.transpose(rounded, (0, 1, 2, 4, 3, 5)).reshape(N_MU, NU_SITE, IG_SZ, BS, PL)
    site_weights = fitting.reshape(SITES, NU_SITE, PL, PL)

    def one_owner(owner_index):
        rows_here = lax.dynamic_index_in_dim(arranged, owner_index, 0, keepdims=False).astype(jnp.float32)
        weights = lax.dynamic_index_in_dim(site_weights, owner_index % SITES, 0, keepdims=False).astype(jnp.float32)
        product = jnp.einsum("kinp,kqp->kinq", rows_here, weights)
        product = product.reshape(NU_SITE, IG_SZ, BS, N_PA, PLS)
        product = jnp.transpose(product, (0, 1, 3, 2, 4)).reshape(NU_SITE, IG_SZ, full_width)
        return product.astype(jnp.bfloat16)

    return lax.map(one_owner, jnp.arange(N_MU, dtype=jnp.int32))
```

```python
import functools

import jax
import jax.numpy as jnp
from jax import lax
from jax.experimental import pallas as pl
from jax.experimental.pallas import tpu as pltpu
from jax.sharding import PartitionSpec as P

SITES = 4
NU_SITE = 12
CAP = 2
SLOTS = SITES * CAP
LANES = 128
CHUNKS = 2
MESH = pl.DeviceIdType.MESH
F32 = jnp.float32
BF16 = jnp.bfloat16


def loop(count, body, carry):
    if count <= 16:
        for step in range(count):
            carry = body(step, carry)
        return carry
    return lax.fori_loop(0, count, body, carry)


def kernel(
    n, mu_ref, site_ref, pos_ref, coeff_ref, tc_hbm, fit_hbm, out_ref,
    tc, fit, turned, payload, arrived, keys_out, keys_in, gath, weights, total,
    tc_sem, fit_sem, key_send, key_recv, pay_send, pay_recv,
    x_send, x_recv, sib_send, sib_recv, fwd_send, fwd_recv,
):
    me = lax.axis_index("mu")
    shard = lax.axis_index("pa")
    sibling = shard + 1 - 2 * lax.rem(shard, 2)
    across = lax.rem(shard + 2, 4)
    diagonal = lax.rem(sibling + 2, 4)
    pairs, block, _ = tc.shape
    width = tc.shape[2] // CHUNKS
    rows = width // LANES
    groups = coeff_ref.shape[1]

    def tc_copy(c):
        columns = pl.ds(c * width, width)
        return pltpu.make_async_copy(
            tc_hbm.at[:, :, columns], tc.at[:, :, columns], tc_sem.at[c]
        )

    for c in range(CHUNKS):
        tc_copy(c).start()
    site = lax.rem(me, SITES)
    fit_copy = pltpu.make_async_copy(
        fit_hbm.at[pl.ds(site * NU_SITE, NU_SITE)], fit, fit_sem
    )
    fit_copy.start()

    barrier = pltpu.get_barrier_semaphore()

    def greet(d, carry):
        pl.semaphore_signal(
            barrier, inc=1, device_id={"mu": lax.rem(me + d + 1, n)}, device_id_type=MESH
        )
        return carry

    loop(n - 1, greet, 0)
    for peer in (sibling, across, diagonal):
        pl.semaphore_signal(barrier, inc=1, device_id={"pa": peer}, device_id_type=MESH)

    slots = []
    for t in range(pairs):
        rank = jnp.int32(0)
        for u in range(t):
            rank += (site_ref[0, u] == site_ref[0, t]).astype(jnp.int32)
        slots.append(site_ref[0, t] * CAP + rank)
    key_row = lax.broadcasted_iota(jnp.int32, (SLOTS, LANES), 0)
    table = jnp.full((SLOTS, LANES), -1.0, F32)
    for t in range(pairs):
        table = jnp.where(key_row == slots[t], pos_ref[0, t].astype(F32), table)
    keys_out[...] = table
    keys_in[0] = table
    slot_row = lax.broadcasted_iota(jnp.int32, (groups, SLOTS, LANES), 1).reshape(
        groups * SLOTS, LANES
    )
    lane = lax.broadcasted_iota(jnp.int32, (groups * SLOTS, LANES), 1)
    halves = []
    for t in range(pairs):
        mu = mu_ref[0, t]
        two = coeff_ref[lax.shift_right_logical(mu, 1)].astype(F32)
        wide = jnp.broadcast_to(two[:, None, :], (groups, SLOTS, LANES))
        wide = wide.reshape(groups * SLOTS, LANES)
        moved = lax.bitwise_and(mu + t, 1) == 1
        wide = jnp.where(moved, pltpu.roll(wide, block, 1), wide)
        halves.append(jnp.where(slot_row == slots[t], wide, 0.0))
    left = []
    for t in range(0, pairs, 2):
        if t + 1 < pairs:
            left.append(jnp.where(lane < block, halves[t], halves[t + 1]).astype(BF16))
        else:
            left.append(halves[t][:, :block].astype(BF16))

    def key_copy(d):
        return pltpu.make_async_remote_copy(
            src_ref=keys_out, dst_ref=keys_in.at[d],
            send_sem=key_send.at[d], recv_sem=key_recv.at[d],
            device_id={"mu": lax.rem(me + d, n)}, device_id_type=MESH,
        )

    def pay_copy(c, d):
        owner = lax.rem(me + d, n)
        return pltpu.make_async_remote_copy(
            src_ref=payload.at[c, owner], dst_ref=arrived.at[c, d],
            send_sem=pay_send.at[c, d], recv_sem=pay_recv.at[c, d],
            device_id={"mu": owner}, device_id_type=MESH,
        )

    def make_payload(c):
        tc_copy(c).wait()
        for j in range(0, rows, 2):
            start = c * width + j * LANES
            acc = None
            for t, part in zip(range(0, pairs, 2), left):
                depth = part.shape[1]
                right = tc[t:t + depth // block, :, start:start + 2 * LANES]
                term = jnp.dot(
                    part, right.reshape(depth, 2 * LANES), preferred_element_type=F32
                )
                acc = term if acc is None else acc + term
            turned[pl.ds(j, n * CAP, stride=rows), :] = acc[:, :LANES]
            turned[pl.ds(j + 1, n * CAP, stride=rows), :] = acc[:, LANES:]

        def pack(w, carry):
            first = w * CAP * rows
            if not isinstance(w, int):
                first = pl.multiple_of(first, CAP * rows)
            payload[c, w] = turned[pl.ds(first, CAP * rows), :].astype(BF16)
            return carry

        loop(n, pack, 0)
        arrived[c, 0] = payload[c, me]

    order = list(range(1, n))
    if n <= 16:
        order.sort(key=lambda d: abs(d - n // 2))

    def each_peer(act):
        if n <= 16:
            for d in order:
                act(d)
        else:
            def body(d, carry):
                act(d)
                return carry
            lax.fori_loop(1, n, body, 0)

    for c in range(CHUNKS):
        make_payload(c)
        if c == 0:
            pl.semaphore_wait(barrier, n - 1 + 3)
            each_peer(lambda d: key_copy(d).start())
        each_peer(lambda d, c=c: pay_copy(c, d).start())

    fit_copy.wait()
    for k in range(NU_SITE):
        double = jnp.concatenate([fit[k], fit[k]], axis=0)
        flipped = double.T
        lane_w = lax.broadcasted_iota(jnp.int32, (block, 2 * block), 1)
        for q in range(4):
            piece = flipped[q * block:(q + 1) * block, :]
            zero = jnp.zeros_like(piece)
            weights[k, q, 0:block, :] = jnp.where(lane_w < block, piece, zero)
            weights[k, q, block:2 * block, :] = jnp.where(lane_w < block, zero, piece)

    each_peer(lambda d: key_copy(d).wait_recv())

    def pa_copy(c, which, target, send, recv):
        return pltpu.make_async_remote_copy(
            src_ref=gath.at[c, which], dst_ref=gath.at[c, which],
            send_sem=send.at[c], recv_sem=recv.at[c],
            device_id={"pa": target}, device_id_type=MESH,
        )

    def x_copy(c):
        return pa_copy(c, shard, across, x_send, x_recv)

    def sib_copy(c):
        return pa_copy(c, shard, sibling, sib_send, sib_recv)

    def fwd_copy(c):
        return pa_copy(c, across, sibling, fwd_send, fwd_recv)

    for c in range(CHUNKS):
        def add_source(d, sums, c=c):
            if n > 16 or d:
                pass
            sums = list(sums)
            for cap in range(CAP):
                key = keys_in[d, pl.ds(site * CAP + cap, 1), :]
                value = arrived[c, d, cap * rows:(cap + 1) * rows, :].astype(F32)
                for k in range(NU_SITE):
                    sums[k] = sums[k] + jnp.where(key == float(k), value, 0.0)
            return tuple(sums)

        sums = tuple(jnp.zeros((rows, LANES), F32) for _ in range(NU_SITE))
        if n <= 16:
            sums = add_source(0, sums)
            for d in reversed(order):
                pay_copy(c, d).wait_recv()
                sums = add_source(d, sums)
        else:
            each_peer(lambda d, c=c: pay_copy(c, d).wait_recv())
            sums = lax.fori_loop(0, n, add_source, sums)
        for k in range(NU_SITE):
            gath[c, shard, k] = sums[k].astype(BF16)
        x_copy(c).start()
        sib_copy(c).start()

    def product(k, chip):
        lines = [
            jnp.concatenate([gath[c, 2 * chip, k], gath[c, 2 * chip + 1, k]], axis=1)
            for c in range(CHUNKS)
        ]
        held = weights[k, pl.ds(2 * chip, 2)].reshape(4 * block, LANES)
        return jnp.dot(jnp.concatenate(lines, axis=0), held, preferred_element_type=F32)

    chip = lax.div(shard, 2)
    for c in range(CHUNKS):
        x_copy(c).wait_recv()
        fwd_copy(c).start()
        sib_copy(c).wait_recv()
    for k in range(NU_SITE):
        total[k] = product(k, chip)
    for c in range(CHUNKS):
        fwd_copy(c).wait_recv()
    for k in range(NU_SITE):
        out_ref[k] = (total[k] + product(k, 1 - chip)).astype(BF16)

    each_peer(lambda d: key_copy(d).wait_send())
    for c in range(CHUNKS):
        each_peer(lambda d, c=c: pay_copy(c, d).wait_send())
        x_copy(c).wait_send()
        sib_copy(c).wait_send()
        fwd_copy(c).wait_send()


def local(three_center, pair_mu, pair_site, pair_pos, coeff, fitting):
    n = lax.axis_size("mu")
    pairs, block, columns = three_center.shape
    orbitals = coeff.shape[1]
    shards = lax.axis_size("pa")
    rows = columns // CHUNKS // LANES
    pair_blocks = coeff.reshape(coeff.shape[0] // LANES, LANES, orbitals).transpose(0, 2, 1)
    smem = pl.BlockSpec(memory_space=pltpu.SMEM)
    vmem = pl.BlockSpec(memory_space=pltpu.VMEM)
    hbm = pl.BlockSpec(memory_space=pltpu.HBM)
    dma = pltpu.SemaphoreType.DMA
    result = pl.pallas_call(
        functools.partial(kernel, n),
        out_shape=jax.ShapeDtypeStruct((NU_SITE, columns // LANES, LANES), BF16),
        in_specs=[smem, smem, smem, vmem, hbm, hbm],
        out_specs=vmem,
        scratch_shapes=[
            pltpu.VMEM((pairs, block, columns), BF16),
            pltpu.VMEM((NU_SITE,) + fitting.shape[1:], BF16),
            pltpu.VMEM((n * CAP * rows, LANES), F32),
            pltpu.VMEM((CHUNKS, n, CAP * rows, LANES), BF16),
            pltpu.VMEM((CHUNKS, n, CAP * rows, LANES), BF16),
            pltpu.VMEM((SLOTS, LANES), F32),
            pltpu.VMEM((n, SLOTS, LANES), F32),
            pltpu.VMEM((CHUNKS, shards, NU_SITE, rows, LANES), BF16),
            pltpu.VMEM((NU_SITE, shards, 2 * block, LANES), BF16),
            pltpu.VMEM((NU_SITE, columns // LANES, LANES), F32),
            dma((CHUNKS,)), dma,
            dma((n,)), dma((n,)), dma((CHUNKS, n)), dma((CHUNKS, n)),
            dma((CHUNKS,)), dma((CHUNKS,)), dma((CHUNKS,)),
            dma((CHUNKS,)), dma((CHUNKS,)), dma((CHUNKS,)),
        ],
        compiler_params=pltpu.CompilerParams(
            collective_id=0, has_side_effects=True, vmem_limit_bytes=40 * 1024 * 1024
        ),
    )(pair_mu, pair_site[:, :, 0], pair_pos, pair_blocks, three_center, fitting)
    shape = (NU_SITE, CHUNKS * rows * LANES)
    return result.reshape((1, NU_SITE, 1, shape[1]))


def solution(mesh):
    in_specs = (
        P("mu", None, "pa"),
        P("mu", None),
        P("mu", None, None),
        P("mu", None),
        P(),
        P(None, "pa", None),
    )
    out_specs = P("mu", None, None, "pa")
    return jax.shard_map(local, mesh=mesh, in_specs=in_specs, out_specs=out_specs, check_vma=False)
```

```python
import functools

import jax
import jax.numpy as jnp
from jax import lax
from jax.experimental import pallas as pl
from jax.experimental.pallas import tpu as pltpu
from jax.sharding import PartitionSpec as P

SITES = 4
NU_SITE = 12
CAP = 2
SLOTS = SITES * CAP
LANES = 128
CHUNKS = 2
VMEM_BYTES = 60 * 1000000
MESH = pl.DeviceIdType.MESH
F32 = jnp.float32
BF16 = jnp.bfloat16


def loop(count, body, carry):
    if count <= 16:
        for step in range(count):
            carry = body(step, carry)
        return carry
    return lax.fori_loop(0, count, body, carry)


def kernel(
    n, mu_hbm, site_hbm, pos_hbm, coeff_hbm, tc_hbm, fit_hbm, out_ref,
    mu_ref, site_ref, pos_ref, coeff_ref, tc, fit, turned, payload, arrived, keys_out, keys_in, gath, weights, total,
    small_sem, tc_sem, fit_sem, key_send, key_recv, pay_send, pay_recv,
    x_send, x_recv, sib_send, sib_recv, fwd_send, fwd_recv,
):
    me = lax.axis_index("mu")
    shard = lax.axis_index("pa")
    sibling = shard + 1 - 2 * lax.rem(shard, 2)
    across = lax.rem(shard + 2, 4)
    diagonal = lax.rem(sibling + 2, 4)
    pairs, block, _ = tc.shape
    width = tc.shape[2] // CHUNKS
    rows = width // LANES
    groups = coeff_ref.shape[1]

    def tc_copy(c):
        columns = pl.ds(c * width, width)
        return pltpu.make_async_copy(
            tc_hbm.at[:, :, columns], tc.at[:, :, columns], tc_sem.at[c]
        )

    small = [
        pltpu.make_async_copy(source, target, small_sem.at[i])
        for i, (source, target) in enumerate((
            (mu_hbm, mu_ref), (site_hbm, site_ref), (pos_hbm, pos_ref), (coeff_hbm, coeff_ref),
        ))
    ]
    for copy in small:
        copy.start()
    for c in range(CHUNKS):
        tc_copy(c).start()
    site = lax.rem(me, SITES)
    fit_copy = pltpu.make_async_copy(
        fit_hbm.at[pl.ds(site * NU_SITE, NU_SITE)], fit, fit_sem
    )
    fit_copy.start()

    barrier = pltpu.get_barrier_semaphore()

    def greet(d, carry):
        pl.semaphore_signal(
            barrier, inc=1, device_id={"mu": lax.rem(me + d + 1, n)}, device_id_type=MESH
        )
        return carry

    loop(n - 1, greet, 0)
    for peer in (sibling, across, diagonal):
        pl.semaphore_signal(barrier, inc=1, device_id={"pa": peer}, device_id_type=MESH)

    for copy in small:
        copy.wait()
    slots = []
    for t in range(pairs):
        rank = jnp.int32(0)
        for u in range(t):
            rank += (site_ref[0, u] == site_ref[0, t]).astype(jnp.int32)
        slots.append(site_ref[0, t] * CAP + rank)
    key_row = lax.broadcasted_iota(jnp.int32, (SLOTS, LANES), 0)
    table = jnp.full((SLOTS, LANES), -1.0, F32)
    for t in range(pairs):
        table = jnp.where(key_row == slots[t], pos_ref[0, t].astype(F32), table)
    first_half = lax.broadcasted_iota(jnp.int32, (1, LANES), 1) < block
    for s in range(SITES):
        keys_out[s] = jnp.where(
            first_half, table[s * CAP:s * CAP + 1, :], table[s * CAP + 1:s * CAP + 2, :]
        )
    keys_in[0] = keys_out[site]
    slot_row = lax.broadcasted_iota(jnp.int32, (groups, SLOTS, LANES), 1).reshape(
        groups * SLOTS, LANES
    )
    lane = lax.broadcasted_iota(jnp.int32, (groups * SLOTS, LANES), 1)
    halves = []
    for t in range(pairs):
        mu = mu_ref[0, t]
        two = coeff_ref[lax.shift_right_logical(mu, 1)].astype(F32)
        wide = jnp.broadcast_to(two[:, None, :], (groups, SLOTS, LANES))
        wide = wide.reshape(groups * SLOTS, LANES)
        moved = lax.bitwise_and(mu + t, 1) == 1
        wide = jnp.where(moved, pltpu.roll(wide, block, 1), wide)
        halves.append(jnp.where(slot_row == slots[t], wide, 0.0))
    left = []
    for t in range(0, pairs, 2):
        if t + 1 < pairs:
            left.append(jnp.where(lane < block, halves[t], halves[t + 1]).astype(BF16))
        else:
            left.append(halves[t][:, :block].astype(BF16))

    def key_copy(d):
        return pltpu.make_async_remote_copy(
            src_ref=keys_out.at[lax.rem(lax.rem(me + d, n), SITES)], dst_ref=keys_in.at[d],
            send_sem=key_send.at[d], recv_sem=key_recv.at[d],
            device_id={"mu": lax.rem(me + d, n)}, device_id_type=MESH,
        )

    def pay_copy(c, d):
        owner = lax.rem(me + d, n)
        return pltpu.make_async_remote_copy(
            src_ref=payload.at[c, owner], dst_ref=arrived.at[c, d],
            send_sem=pay_send.at[c, d], recv_sem=pay_recv.at[c, d],
            device_id={"mu": owner}, device_id_type=MESH,
        )

    def make_payload(c):
        tc_copy(c).wait()
        for j in range(0, rows, 2):
            start = c * width + j * LANES
            acc = None
            for t, part in zip(range(0, pairs, 2), left):
                depth = part.shape[1]
                right = tc[t:t + depth // block, :, start:start + 2 * LANES]
                term = jnp.dot(
                    part, right.reshape(depth, 2 * LANES), preferred_element_type=F32
                )
                acc = term if acc is None else acc + term
            turned[pl.ds(j, n * CAP, stride=rows), :] = acc[:, :LANES]
            turned[pl.ds(j + 1, n * CAP, stride=rows), :] = acc[:, LANES:]

        def pack(w, carry):
            first = w * CAP * rows
            if not isinstance(w, int):
                first = pl.multiple_of(first, CAP * rows)
            payload[c, w] = turned[pl.ds(first, CAP * rows), :].astype(BF16)
            return carry

        loop(n, pack, 0)
        arrived[c, 0] = payload[c, me]

    order = list(range(1, n))
    if n <= 16:
        order.sort(key=lambda d: abs(d - n // 2))

    def each_peer(act):
        if n <= 16:
            for d in order:
                act(d)
        else:
            def body(d, carry):
                act(d)
                return carry
            lax.fori_loop(1, n, body, 0)

    for c in range(CHUNKS):
        make_payload(c)
        if c == 0:
            pl.semaphore_wait(barrier, n - 1 + 3)
            each_peer(lambda d: key_copy(d).start())
        each_peer(lambda d, c=c: pay_copy(c, d).start())

    fit_copy.wait()
    for k in range(NU_SITE):
        double = jnp.concatenate([fit[k], fit[k]], axis=0)
        flipped = double.T
        lane_w = lax.broadcasted_iota(jnp.int32, (block, 2 * block), 1)
        for q in range(4):
            piece = flipped[q * block:(q + 1) * block, :]
            zero = jnp.zeros_like(piece)
            weights[k, q, 0:block, :] = jnp.where(lane_w < block, piece, zero)
            weights[k, q, block:2 * block, :] = jnp.where(lane_w < block, zero, piece)

    each_peer(lambda d: key_copy(d).wait_recv())

    def pa_copy(c, which, target, send, recv):
        return pltpu.make_async_remote_copy(
            src_ref=gath.at[c, which], dst_ref=gath.at[c, which],
            send_sem=send.at[c], recv_sem=recv.at[c],
            device_id={"pa": target}, device_id_type=MESH,
        )

    def x_copy(c):
        return pa_copy(c, shard, across, x_send, x_recv)

    def sib_copy(c):
        return pa_copy(c, shard, sibling, sib_send, sib_recv)

    def fwd_copy(c):
        return pa_copy(c, across, sibling, fwd_send, fwd_recv)

    for c in range(CHUNKS):
        def add_source(d, sums, c=c):
            sums = list(sums)
            both = keys_in[d]
            other = pltpu.roll(both, block, 1)
            for cap in range(CAP):
                key = jnp.where(first_half, *((both, other) if cap == 0 else (other, both)))
                value = arrived[c, d, cap * rows:(cap + 1) * rows, :].astype(F32)
                for k in range(NU_SITE):
                    sums[k] = sums[k] + jnp.where(key == float(k), value, 0.0)
            return tuple(sums)

        sums = tuple(jnp.zeros((rows, LANES), F32) for _ in range(NU_SITE))
        if n <= 16:
            sums = add_source(0, sums)
            for d in reversed(order):
                pay_copy(c, d).wait_recv()
                sums = add_source(d, sums)
        else:
            each_peer(lambda d, c=c: pay_copy(c, d).wait_recv())
            sums = lax.fori_loop(0, n, add_source, sums)
        for k in range(NU_SITE):
            gath[c, shard, k] = sums[k].astype(BF16)
        x_copy(c).start()
        sib_copy(c).start()

    def product(k, chip):
        lines = [
            jnp.concatenate([gath[c, 2 * chip, k], gath[c, 2 * chip + 1, k]], axis=1)
            for c in range(CHUNKS)
        ]
        held = weights[k, pl.ds(2 * chip, 2)].reshape(4 * block, LANES)
        return jnp.dot(jnp.concatenate(lines, axis=0), held, preferred_element_type=F32)

    chip = lax.div(shard, 2)
    for c in range(CHUNKS):
        x_copy(c).wait_recv()
        fwd_copy(c).start()
        sib_copy(c).wait_recv()
    for k in range(NU_SITE):
        total[k] = product(k, chip)
    for c in range(CHUNKS):
        fwd_copy(c).wait_recv()
    for k in range(NU_SITE):
        out_ref[k] = (total[k] + product(k, 1 - chip)).astype(BF16)

    each_peer(lambda d: key_copy(d).wait_send())
    for c in range(CHUNKS):
        each_peer(lambda d, c=c: pay_copy(c, d).wait_send())
        x_copy(c).wait_send()
        sib_copy(c).wait_send()
        fwd_copy(c).wait_send()


def local(three_center, pair_mu, pair_site, pair_pos, coeff, fitting):
    n = lax.axis_size("mu")
    pairs, block, columns = three_center.shape
    orbitals = coeff.shape[1]
    shards = lax.axis_size("pa")
    rows = columns // CHUNKS // LANES
    pair_blocks = coeff.reshape(coeff.shape[0] // LANES, LANES, orbitals).transpose(0, 2, 1)
    vmem = pl.BlockSpec(memory_space=pltpu.VMEM)
    hbm = pl.BlockSpec(memory_space=pltpu.HBM)
    dma = pltpu.SemaphoreType.DMA
    result = pl.pallas_call(
        functools.partial(kernel, n),
        out_shape=jax.ShapeDtypeStruct((NU_SITE, columns // LANES, LANES), BF16),
        in_specs=[hbm] * 6,
        out_specs=vmem,
        scratch_shapes=[
            pltpu.SMEM((1, pairs), jnp.int32),
            pltpu.SMEM((1, pairs), jnp.int32),
            pltpu.SMEM((1, pairs), jnp.int32),
            pltpu.VMEM(pair_blocks.shape, BF16),
            pltpu.VMEM((pairs, block, columns), BF16),
            pltpu.VMEM((NU_SITE,) + fitting.shape[1:], BF16),
            pltpu.VMEM((n * CAP * rows, LANES), F32),
            pltpu.VMEM((CHUNKS, n, CAP * rows, LANES), BF16),
            pltpu.VMEM((CHUNKS, n, CAP * rows, LANES), BF16),
            pltpu.VMEM((SITES, 1, LANES), F32),
            pltpu.VMEM((n, 1, LANES), F32),
            pltpu.VMEM((CHUNKS, shards, NU_SITE, rows, LANES), BF16),
            pltpu.VMEM((NU_SITE, shards, 2 * block, LANES), BF16),
            pltpu.VMEM((NU_SITE, columns // LANES, LANES), F32),
            dma((4,)), dma((CHUNKS,)), dma,
            dma((n,)), dma((n,)), dma((CHUNKS, n)), dma((CHUNKS, n)),
            dma((CHUNKS,)), dma((CHUNKS,)), dma((CHUNKS,)),
            dma((CHUNKS,)), dma((CHUNKS,)), dma((CHUNKS,)),
        ],
        compiler_params=pltpu.CompilerParams(
            collective_id=0, has_side_effects=True, vmem_limit_bytes=VMEM_BYTES
        ),
    )(pair_mu, pair_site[:, :, 0], pair_pos, pair_blocks, three_center, fitting)
    shape = (NU_SITE, CHUNKS * rows * LANES)
    return result.reshape((1, NU_SITE, 1, shape[1]))


def solution(mesh):
    in_specs = (
        P("mu", None, "pa"),
        P("mu", None),
        P("mu", None, None),
        P("mu", None),
        P(),
        P(None, "pa", None),
    )
    out_specs = P("mu", None, None, "pa")
    return jax.shard_map(local, mesh=mesh, in_specs=in_specs, out_specs=out_specs, check_vma=False)
```

```python
import functools

import jax
import jax.numpy as jnp
from jax import lax
from jax.experimental import pallas as pl
from jax.experimental.pallas import tpu as pltpu
from jax.sharding import PartitionSpec as P

SITES = 4
NU_SITE = 12
CAP = 2
SLOTS = SITES * CAP
LANES = 128
CHUNKS = 2
VMEM_BYTES = 60 * 1000000
MESH = pl.DeviceIdType.MESH
F32 = jnp.float32
BF16 = jnp.bfloat16


def loop(count, body, carry):
    if count <= 16:
        for step in range(count):
            carry = body(step, carry)
        return carry
    return lax.fori_loop(0, count, body, carry)


def kernel(
    n, mu_hbm, site_hbm, pos_hbm, coeff_hbm, tc_hbm, fit_hbm, out_ref,
    mu_ref, site_ref, pos_ref, coeff_ref, tc, fit, turned, payload, arrived, keys_out, keys_in, gath, weights, total, spread,
    small_sem, tc_sem, fit_sem, key_send, key_recv, pay_send, pay_recv,
    x_send, x_recv, sib_send, sib_recv, fwd_send, fwd_recv,
):
    me = lax.axis_index("mu")
    shard = lax.axis_index("pa")
    sibling = shard + 1 - 2 * lax.rem(shard, 2)
    across = lax.rem(shard + 2, 4)
    diagonal = lax.rem(sibling + 2, 4)
    pairs, block, _ = tc.shape
    width = tc.shape[2] // CHUNKS
    rows = width // LANES
    groups = coeff_ref.shape[1]

    def tc_copy(c):
        columns = pl.ds(c * width, width)
        return pltpu.make_async_copy(
            tc_hbm.at[:, :, columns], tc.at[:, :, columns], tc_sem.at[c]
        )

    small = [
        pltpu.make_async_copy(source, target, small_sem.at[i])
        for i, (source, target) in enumerate((
            (mu_hbm, mu_ref), (site_hbm, site_ref), (pos_hbm, pos_ref), (coeff_hbm, coeff_ref),
        ))
    ]
    for copy in small:
        copy.start()
    for c in range(CHUNKS):
        tc_copy(c).start()
    site = lax.rem(me, SITES)
    fit_copy = pltpu.make_async_copy(
        fit_hbm.at[pl.ds(site * NU_SITE, NU_SITE)], fit, fit_sem
    )
    fit_copy.start()

    barrier = pltpu.get_barrier_semaphore()

    def greet(d, carry):
        pl.semaphore_signal(
            barrier, inc=1, device_id={"mu": lax.rem(me + d + 1, n)}, device_id_type=MESH
        )
        return carry

    loop(n - 1, greet, 0)
    for peer in (sibling, across, diagonal):
        pl.semaphore_signal(barrier, inc=1, device_id={"pa": peer}, device_id_type=MESH)

    for copy in small:
        copy.wait()
    slots = []
    for t in range(pairs):
        rank = jnp.int32(0)
        for u in range(t):
            rank += (site_ref[0, u] == site_ref[0, t]).astype(jnp.int32)
        slots.append(site_ref[0, t] * CAP + rank)
    key_row = lax.broadcasted_iota(jnp.int32, (SLOTS, LANES), 0)
    table = jnp.full((SLOTS, LANES), -1.0, F32)
    for t in range(pairs):
        table = jnp.where(key_row == slots[t], pos_ref[0, t].astype(F32), table)
    first_half = lax.broadcasted_iota(jnp.int32, (1, LANES), 1) < block
    for s in range(SITES):
        keys_out[s] = jnp.where(
            first_half, table[s * CAP:s * CAP + 1, :], table[s * CAP + 1:s * CAP + 2, :]
        )
    keys_in[0] = keys_out[site]
    slot_row = lax.broadcasted_iota(jnp.int32, (groups, SLOTS, LANES), 1).reshape(
        groups * SLOTS, LANES
    )
    lane = lax.broadcasted_iota(jnp.int32, (groups * SLOTS, LANES), 1)
    halves = []
    for t in range(pairs):
        mu = mu_ref[0, t]
        two = coeff_ref[lax.shift_right_logical(mu, 1)].astype(F32)
        wide = jnp.broadcast_to(two[:, None, :], (groups, SLOTS, LANES))
        wide = wide.reshape(groups * SLOTS, LANES)
        moved = lax.bitwise_and(mu + t, 1) == 1
        wide = jnp.where(moved, pltpu.roll(wide, block, 1), wide)
        halves.append(jnp.where(slot_row == slots[t], wide, 0.0))
    left = []
    for t in range(0, pairs, 2):
        if t + 1 < pairs:
            left.append(jnp.where(lane < block, halves[t], halves[t + 1]).astype(BF16))
        else:
            left.append(halves[t][:, :block].astype(BF16))

    def key_copy(d):
        return pltpu.make_async_remote_copy(
            src_ref=keys_out.at[lax.rem(lax.rem(me + d, n), SITES)], dst_ref=keys_in.at[d],
            send_sem=key_send.at[d], recv_sem=key_recv.at[d],
            device_id={"mu": lax.rem(me + d, n)}, device_id_type=MESH,
        )

    def pay_copy(c, d):
        owner = lax.rem(me + d, n)
        return pltpu.make_async_remote_copy(
            src_ref=payload.at[c, owner], dst_ref=arrived.at[c, d],
            send_sem=pay_send.at[c, d], recv_sem=pay_recv.at[c, d],
            device_id={"mu": owner}, device_id_type=MESH,
        )

    def make_payload(c):
        tc_copy(c).wait()
        for j in range(0, rows, 2):
            start = c * width + j * LANES
            acc = None
            for t, part in zip(range(0, pairs, 2), left):
                depth = part.shape[1]
                right = tc[t:t + depth // block, :, start:start + 2 * LANES]
                term = jnp.dot(
                    part, right.reshape(depth, 2 * LANES), preferred_element_type=F32
                )
                acc = term if acc is None else acc + term
            turned[pl.ds(j, n * CAP, stride=rows), :] = acc[:, :LANES]
            turned[pl.ds(j + 1, n * CAP, stride=rows), :] = acc[:, LANES:]

        def pack(w, carry):
            first = w * CAP * rows
            if not isinstance(w, int):
                first = pl.multiple_of(first, CAP * rows)
            payload[c, w] = turned[pl.ds(first, CAP * rows), :].astype(BF16)
            return carry

        loop(n, pack, 0)
        arrived[c, 0] = payload[c, me]

    order = list(range(1, n))
    if n <= 16:
        order.sort(key=lambda d: abs(d - n // 2))

    def each_peer(act):
        if n <= 16:
            for d in order:
                act(d)
        else:
            def body(d, carry):
                act(d)
                return carry
            lax.fori_loop(1, n, body, 0)

    for c in range(CHUNKS):
        make_payload(c)
        if c == 0:
            pl.semaphore_wait(barrier, n - 1 + 3)
            each_peer(lambda d: key_copy(d).start())
        each_peer(lambda d, c=c: pay_copy(c, d).start())

    fit_copy.wait()
    for k in range(NU_SITE):
        double = jnp.concatenate([fit[k], fit[k]], axis=0)
        flipped = double.T
        lane_w = lax.broadcasted_iota(jnp.int32, (block, 2 * block), 1)
        for q in range(4):
            piece = flipped[q * block:(q + 1) * block, :]
            zero = jnp.zeros_like(piece)
            weights[k, q, 0:block, :] = jnp.where(lane_w < block, piece, zero)
            weights[k, q, block:2 * block, :] = jnp.where(lane_w < block, zero, piece)

    each_peer(lambda d: key_copy(d).wait_recv())

    def pa_copy(c, which, target, send, recv):
        return pltpu.make_async_remote_copy(
            src_ref=gath.at[c, which], dst_ref=gath.at[c, which],
            send_sem=send.at[c], recv_sem=recv.at[c],
            device_id={"pa": target}, device_id_type=MESH,
        )

    def x_copy(c):
        return pa_copy(c, shard, across, x_send, x_recv)

    def sib_copy(c):
        return pa_copy(c, shard, sibling, sib_send, sib_recv)

    def fwd_copy(c):
        return pa_copy(c, across, sibling, fwd_send, fwd_recv)

    for c in range(CHUNKS):
        def add_source(d, sums, c=c):
            sums = list(sums)
            both = keys_in[d]
            other = pltpu.roll(both, block, 1)
            for cap in range(CAP):
                key = jnp.where(first_half, *((both, other) if cap == 0 else (other, both)))
                value = arrived[c, d, cap * rows:(cap + 1) * rows, :].astype(F32)
                for k in range(NU_SITE):
                    sums[k] = sums[k] + jnp.where(key == float(k), value, 0.0)
            return tuple(sums)

        sums = tuple(jnp.zeros((rows, LANES), F32) for _ in range(NU_SITE))
        if n <= 16:
            sums = add_source(0, sums)
            for d in reversed(order):
                pay_copy(c, d).wait_recv()
                sums = add_source(d, sums)
        else:
            each_peer(lambda d, c=c: pay_copy(c, d).wait_recv())
            sums = lax.fori_loop(0, n, add_source, sums)
        for k in range(NU_SITE):
            gath[c, shard, k * rows:(k + 1) * rows, :] = sums[k].astype(BF16)
        x_copy(c).start()
        sib_copy(c).start()

    def lines(k, which):
        return jnp.concatenate(
            [gath[c, which, k * rows:(k + 1) * rows, :] for c in range(CHUNKS)], axis=0
        )

    def product(k, which):
        return jnp.dot(lines(k, which), weights[k, which], preferred_element_type=F32)

    for c in range(CHUNKS):
        sib_copy(c).wait_recv()
    first = 2 * lax.div(shard, 2)
    for k in range(NU_SITE):
        pair = jnp.concatenate([lines(k, first), lines(k, first + 1)], axis=1)
        held = weights[k, pl.ds(first, 2)].reshape(4 * block, LANES)
        total[k] = jnp.dot(pair, held, preferred_element_type=F32)
    for c in range(CHUNKS):
        x_copy(c).wait_recv()
        fwd_copy(c).start()
    for k in range(NU_SITE):
        total[k] += product(k, across)
    for c in range(CHUNKS):
        fwd_copy(c).wait_recv()
    for k in range(NU_SITE):
        spread[pl.ds(k, CHUNKS * rows, stride=16), :] = total[k] + product(k, diagonal)
    for j in range(CHUNKS * rows):
        out_ref[:, j * LANES:(j + 1) * LANES] = spread[j * 16:j * 16 + NU_SITE, :].astype(BF16)

    each_peer(lambda d: key_copy(d).wait_send())
    for c in range(CHUNKS):
        each_peer(lambda d, c=c: pay_copy(c, d).wait_send())
        x_copy(c).wait_send()
        sib_copy(c).wait_send()
        fwd_copy(c).wait_send()


def local(three_center, pair_mu, pair_site, pair_pos, coeff, fitting):
    n = lax.axis_size("mu")
    pairs, block, columns = three_center.shape
    orbitals = coeff.shape[1]
    shards = lax.axis_size("pa")
    rows = columns // CHUNKS // LANES
    pair_blocks = coeff.reshape(coeff.shape[0] // LANES, LANES, orbitals).transpose(0, 2, 1)
    vmem = pl.BlockSpec(memory_space=pltpu.VMEM)
    hbm = pl.BlockSpec(memory_space=pltpu.HBM)
    dma = pltpu.SemaphoreType.DMA
    result = pl.pallas_call(
        functools.partial(kernel, n),
        out_shape=jax.ShapeDtypeStruct((NU_SITE, columns), BF16),
        in_specs=[hbm] * 6,
        out_specs=vmem,
        scratch_shapes=[
            pltpu.SMEM((1, pairs), jnp.int32),
            pltpu.SMEM((1, pairs), jnp.int32),
            pltpu.SMEM((1, pairs), jnp.int32),
            pltpu.VMEM(pair_blocks.shape, BF16),
            pltpu.VMEM((pairs, block, columns), BF16),
            pltpu.VMEM((NU_SITE,) + fitting.shape[1:], BF16),
            pltpu.VMEM((n * CAP * rows, LANES), F32),
            pltpu.VMEM((CHUNKS, n, CAP * rows, LANES), BF16),
            pltpu.VMEM((CHUNKS, n, CAP * rows, LANES), BF16),
            pltpu.VMEM((SITES, 1, LANES), F32),
            pltpu.VMEM((n, 1, LANES), F32),
            pltpu.VMEM((CHUNKS, shards, NU_SITE * rows, LANES), BF16),
            pltpu.VMEM((NU_SITE, shards, 2 * block, LANES), BF16),
            pltpu.VMEM((NU_SITE, columns // LANES, LANES), F32),
            pltpu.VMEM((columns // LANES * 16, LANES), F32),
            dma((4,)), dma((CHUNKS,)), dma,
            dma((n,)), dma((n,)), dma((CHUNKS, n)), dma((CHUNKS, n)),
            dma((CHUNKS,)), dma((CHUNKS,)), dma((CHUNKS,)),
            dma((CHUNKS,)), dma((CHUNKS,)), dma((CHUNKS,)),
        ],
        compiler_params=pltpu.CompilerParams(
            collective_id=0, has_side_effects=True, vmem_limit_bytes=VMEM_BYTES
        ),
    )(pair_mu, pair_site[:, :, 0], pair_pos, pair_blocks, three_center, fitting)
    return result.reshape((1, NU_SITE, 1, columns))


def solution(mesh):
    in_specs = (
        P("mu", None, "pa"),
        P("mu", None),
        P("mu", None, None),
        P("mu", None),
        P(),
        P(None, "pa", None),
    )
    out_specs = P("mu", None, None, "pa")
    return jax.shard_map(local, mesh=mesh, in_specs=in_specs, out_specs=out_specs, check_vma=False)
```

```python
import functools

import jax
import jax.numpy as jnp
from jax import lax
from jax.experimental import pallas as pl
from jax.experimental.pallas import tpu as pltpu
from jax.sharding import PartitionSpec as P

SITES = 4
NU_SITE = 12
CAP = 2
SLOTS = SITES * CAP
LANES = 128
CHUNKS = 2
VMEM_BYTES = 40 * 1024 * 1024
MESH = pl.DeviceIdType.MESH
F32 = jnp.float32
BF16 = jnp.bfloat16


def loop(count, body, carry):
    if count <= 16:
        for step in range(count):
            carry = body(step, carry)
        return carry
    return lax.fori_loop(0, count, body, carry)


def kernel(
    n, mu_hbm, site_hbm, pos_hbm, coeff_hbm, tc_hbm, fit_hbm, out_ref,
    mu_ref, site_ref, pos_ref, coeff_ref, tc, fit, turned, payload, arrived, keys_out, keys_in, gath, weights, total, spread,
    small_sem, tc_sem, fit_sem, key_send, key_recv, pay_send, pay_recv,
    x_send, x_recv, sib_send, sib_recv, fwd_send, fwd_recv,
):
    me = lax.axis_index("mu")
    shard = lax.axis_index("pa")
    sibling = shard + 1 - 2 * lax.rem(shard, 2)
    across = lax.rem(shard + 2, 4)
    diagonal = lax.rem(sibling + 2, 4)
    pairs, block, _ = tc.shape
    width = tc.shape[2] // CHUNKS
    rows = width // LANES
    groups = coeff_ref.shape[1]

    def tc_copy(c):
        columns = pl.ds(c * width, width)
        return pltpu.make_async_copy(
            tc_hbm.at[:, :, columns], tc.at[:, :, columns], tc_sem.at[c]
        )

    small = [
        pltpu.make_async_copy(source, target, small_sem.at[i])
        for i, (source, target) in enumerate((
            (mu_hbm, mu_ref), (site_hbm, site_ref), (pos_hbm, pos_ref), (coeff_hbm, coeff_ref),
        ))
    ]
    for copy in small:
        copy.start()
    for c in range(CHUNKS):
        tc_copy(c).start()
    site = lax.rem(me, SITES)
    fit_copy = pltpu.make_async_copy(
        fit_hbm.at[pl.ds(site * NU_SITE, NU_SITE)], fit, fit_sem
    )
    fit_copy.start()

    barrier = pltpu.get_barrier_semaphore()

    def greet(d, carry):
        pl.semaphore_signal(
            barrier, inc=1, device_id={"mu": lax.rem(me + d + 1, n)}, device_id_type=MESH
        )
        return carry

    loop(n - 1, greet, 0)
    for peer in (sibling, across, diagonal):
        pl.semaphore_signal(barrier, inc=1, device_id={"pa": peer}, device_id_type=MESH)

    for copy in small:
        copy.wait()
    slots = []
    for t in range(pairs):
        rank = jnp.int32(0)
        for u in range(t):
            rank += (site_ref[0, u] == site_ref[0, t]).astype(jnp.int32)
        slots.append(site_ref[0, t] * CAP + rank)
    key_row = lax.broadcasted_iota(jnp.int32, (SLOTS, LANES), 0)
    table = jnp.full((SLOTS, LANES), -1.0, F32)
    for t in range(pairs):
        table = jnp.where(key_row == slots[t], pos_ref[0, t].astype(F32), table)
    first_half = lax.broadcasted_iota(jnp.int32, (1, LANES), 1) < block
    for s in range(SITES):
        keys_out[s] = jnp.where(
            first_half, table[s * CAP:s * CAP + 1, :], table[s * CAP + 1:s * CAP + 2, :]
        )
    keys_in[0] = keys_out[site]
    slot_row = lax.broadcasted_iota(jnp.int32, (groups, SLOTS, LANES), 1).reshape(
        groups * SLOTS, LANES
    )
    lane = lax.broadcasted_iota(jnp.int32, (groups * SLOTS, LANES), 1)
    halves = []
    for t in range(pairs):
        mu = mu_ref[0, t]
        two = coeff_ref[lax.shift_right_logical(mu, 1)].astype(F32)
        wide = jnp.broadcast_to(two[:, None, :], (groups, SLOTS, LANES))
        wide = wide.reshape(groups * SLOTS, LANES)
        moved = lax.bitwise_and(mu + t, 1) == 1
        wide = jnp.where(moved, pltpu.roll(wide, block, 1), wide)
        halves.append(jnp.where(slot_row == slots[t], wide, 0.0))
    left = []
    for t in range(0, pairs, 2):
        if t + 1 < pairs:
            left.append(jnp.where(lane < block, halves[t], halves[t + 1]).astype(BF16))
        else:
            left.append(halves[t][:, :block].astype(BF16))

    def key_copy(d):
        return pltpu.make_async_remote_copy(
            src_ref=keys_out.at[lax.rem(lax.rem(me + d, n), SITES)], dst_ref=keys_in.at[d],
            send_sem=key_send.at[d], recv_sem=key_recv.at[d],
            device_id={"mu": lax.rem(me + d, n)}, device_id_type=MESH,
        )

    def pay_copy(c, d):
        owner = lax.rem(me + d, n)
        return pltpu.make_async_remote_copy(
            src_ref=payload.at[c, owner], dst_ref=arrived.at[c, d],
            send_sem=pay_send.at[c, d], recv_sem=pay_recv.at[c, d],
            device_id={"mu": owner}, device_id_type=MESH,
        )

    def make_payload(c):
        tc_copy(c).wait()
        for j in range(0, rows, 2):
            start = c * width + j * LANES
            acc = None
            for t, part in zip(range(0, pairs, 2), left):
                depth = part.shape[1]
                right = tc[t:t + depth // block, :, start:start + 2 * LANES]
                term = jnp.dot(
                    part, right.reshape(depth, 2 * LANES), preferred_element_type=F32
                )
                acc = term if acc is None else acc + term
            turned[pl.ds(j, n * CAP, stride=rows), :] = acc[:, :LANES]
            turned[pl.ds(j + 1, n * CAP, stride=rows), :] = acc[:, LANES:]

        def pack(w, carry):
            first = w * CAP * rows
            if not isinstance(w, int):
                first = pl.multiple_of(first, CAP * rows)
            payload[c, w] = turned[pl.ds(first, CAP * rows), :].astype(BF16)
            return carry

        loop(n, pack, 0)
        arrived[c, 0] = payload[c, me]

    order = list(range(1, n))
    if n <= 16:
        order.sort(key=lambda d: abs(d - n // 2))

    def each_peer(act):
        if n <= 16:
            for d in order:
                act(d)
        else:
            def body(d, carry):
                act(d)
                return carry
            lax.fori_loop(1, n, body, 0)

    for c in range(CHUNKS):
        make_payload(c)
        if c == 0:
            pl.semaphore_wait(barrier, n - 1 + 3)
            each_peer(lambda d: key_copy(d).start())
        each_peer(lambda d, c=c: pay_copy(c, d).start())

    fit_copy.wait()
    for k in range(NU_SITE):
        double = jnp.concatenate([fit[k], fit[k]], axis=0)
        flipped = double.T
        lane_w = lax.broadcasted_iota(jnp.int32, (block, 2 * block), 1)
        for q in range(4):
            piece = flipped[q * block:(q + 1) * block, :]
            zero = jnp.zeros_like(piece)
            weights[k, q, 0:block, :] = jnp.where(lane_w < block, piece, zero)
            weights[k, q, block:2 * block, :] = jnp.where(lane_w < block, zero, piece)

    each_peer(lambda d: key_copy(d).wait_recv())

    def pa_copy(c, which, target, send, recv):
        return pltpu.make_async_remote_copy(
            src_ref=gath.at[c, which], dst_ref=gath.at[c, which],
            send_sem=send.at[c], recv_sem=recv.at[c],
            device_id={"pa": target}, device_id_type=MESH,
        )

    def x_copy(c):
        return pa_copy(c, shard, across, x_send, x_recv)

    def sib_copy(c):
        return pa_copy(c, shard, sibling, sib_send, sib_recv)

    def fwd_copy(c):
        return pa_copy(c, across, sibling, fwd_send, fwd_recv)

    for c in range(CHUNKS):
        def add_source(d, sums, c=c):
            sums = list(sums)
            both = keys_in[d]
            other = pltpu.roll(both, block, 1)
            for cap in range(CAP):
                key = jnp.where(first_half, *((both, other) if cap == 0 else (other, both)))
                value = arrived[c, d, cap * rows:(cap + 1) * rows, :].astype(F32)
                for k in range(NU_SITE):
                    sums[k] = sums[k] + jnp.where(key == float(k), value, 0.0)
            return tuple(sums)

        sums = tuple(jnp.zeros((rows, LANES), F32) for _ in range(NU_SITE))
        if n <= 16:
            sums = add_source(0, sums)
            for d in reversed(order):
                pay_copy(c, d).wait_recv()
                sums = add_source(d, sums)
        else:
            each_peer(lambda d, c=c: pay_copy(c, d).wait_recv())
            sums = lax.fori_loop(0, n, add_source, sums)
        for k in range(NU_SITE):
            gath[c, shard, k * rows:(k + 1) * rows, :] = sums[k].astype(BF16)
        x_copy(c).start()
        sib_copy(c).start()

    def lines(k, which):
        return jnp.concatenate(
            [gath[c, which, k * rows:(k + 1) * rows, :] for c in range(CHUNKS)], axis=0
        )

    def product(k, which):
        return jnp.dot(lines(k, which), weights[k, which], preferred_element_type=F32)

    for c in range(CHUNKS):
        sib_copy(c).wait_recv()
    first = 2 * lax.div(shard, 2)
    for k in range(NU_SITE):
        pair = jnp.concatenate([lines(k, first), lines(k, first + 1)], axis=1)
        held = weights[k, pl.ds(first, 2)].reshape(4 * block, LANES)
        total[k] = jnp.dot(pair, held, preferred_element_type=F32)
    for c in range(CHUNKS):
        x_copy(c).wait_recv()
        fwd_copy(c).start()
    for k in range(NU_SITE):
        total[k] += product(k, across)
    for c in range(CHUNKS):
        fwd_copy(c).wait_recv()
    for k in range(NU_SITE):
        spread[pl.ds(k, CHUNKS * rows, stride=16), :] = total[k] + product(k, diagonal)
    for j in range(CHUNKS * rows):
        out_ref[:, j * LANES:(j + 1) * LANES] = spread[j * 16:j * 16 + NU_SITE, :].astype(BF16)

    each_peer(lambda d: key_copy(d).wait_send())
    for c in range(CHUNKS):
        each_peer(lambda d, c=c: pay_copy(c, d).wait_send())
        x_copy(c).wait_send()
        sib_copy(c).wait_send()
        fwd_copy(c).wait_send()


def local(three_center, pair_mu, pair_site, pair_pos, coeff, fitting):
    n = lax.axis_size("mu")
    pairs, block, columns = three_center.shape
    orbitals = coeff.shape[1]
    shards = lax.axis_size("pa")
    rows = columns // CHUNKS // LANES
    pair_blocks = coeff.reshape(coeff.shape[0] // LANES, LANES, orbitals).transpose(0, 2, 1)
    vmem = pl.BlockSpec(memory_space=pltpu.VMEM)
    hbm = pl.BlockSpec(memory_space=pltpu.HBM)
    dma = pltpu.SemaphoreType.DMA
    result = pl.pallas_call(
        functools.partial(kernel, n),
        out_shape=jax.ShapeDtypeStruct((NU_SITE, columns), BF16),
        in_specs=[hbm] * 6,
        out_specs=vmem,
        scratch_shapes=[
            pltpu.SMEM((1, pairs), jnp.int32),
            pltpu.SMEM((1, pairs), jnp.int32),
            pltpu.SMEM((1, pairs), jnp.int32),
            pltpu.VMEM(pair_blocks.shape, BF16),
            pltpu.VMEM((pairs, block, columns), BF16),
            pltpu.VMEM((NU_SITE,) + fitting.shape[1:], BF16),
            pltpu.VMEM((n * CAP * rows, LANES), F32),
            pltpu.VMEM((CHUNKS, n, CAP * rows, LANES), BF16),
            pltpu.VMEM((CHUNKS, n, CAP * rows, LANES), BF16),
            pltpu.VMEM((SITES, 1, LANES), F32),
            pltpu.VMEM((n, 1, LANES), F32),
            pltpu.VMEM((CHUNKS, shards, NU_SITE * rows, LANES), BF16),
            pltpu.VMEM((NU_SITE, shards, 2 * block, LANES), BF16),
            pltpu.VMEM((NU_SITE, columns // LANES, LANES), F32),
            pltpu.VMEM((columns // LANES * 16, LANES), F32),
            dma((4,)), dma((CHUNKS,)), dma,
            dma((n,)), dma((n,)), dma((CHUNKS, n)), dma((CHUNKS, n)),
            dma((CHUNKS,)), dma((CHUNKS,)), dma((CHUNKS,)),
            dma((CHUNKS,)), dma((CHUNKS,)), dma((CHUNKS,)),
        ],
        compiler_params=pltpu.CompilerParams(
            collective_id=0, has_side_effects=True, vmem_limit_bytes=VMEM_BYTES
        ),
    )(*(
        pltpu.with_memory_space_constraint(operand, pltpu.HBM)
        for operand in (
            pair_mu, pair_site[:, :, 0], pair_pos, pair_blocks, three_center, fitting
        )
    ))
    return result.reshape((1, NU_SITE, 1, columns))


def solution(mesh):
    in_specs = (
        P("mu", None, "pa"),
        P("mu", None),
        P("mu", None, None),
        P("mu", None),
        P(),
        P(None, "pa", None),
    )
    out_specs = P("mu", None, None, "pa")
    return jax.shard_map(local, mesh=mesh, in_specs=in_specs, out_specs=out_specs, check_vma=False)
```

```python
import functools

import jax
import jax.numpy as jnp
from jax import lax
from jax.experimental import pallas as pl
from jax.experimental.pallas import tpu as pltpu
from jax.sharding import PartitionSpec as P

SITES = 4
NU_SITE = 12
CAP = 2
SLOTS = SITES * CAP
LANES = 128
CHUNKS = 2
VMEM_BYTES = 40 * 1024 * 1024
MESH = pl.DeviceIdType.MESH
F32 = jnp.float32
BF16 = jnp.bfloat16


def loop(count, body, carry):
    if count <= 16:
        for step in range(count):
            carry = body(step, carry)
        return carry
    return lax.fori_loop(0, count, body, carry)


def kernel(
    n, mu_hbm, site_hbm, pos_hbm, coeff_hbm, tc_hbm, fit_hbm, out_ref,
    mu_ref, site_ref, pos_ref, coeff_ref, tc, fit, turned, payload, arrived, keys_out, keys_in, gath, total, spread,
    small_sem, tc_sem, fit_sem, key_send, key_recv, pay_send, pay_recv,
    x_send, x_recv, sib_send, sib_recv, fwd_send, fwd_recv,
):
    me = lax.axis_index("mu")
    shard = lax.axis_index("pa")
    sibling = shard + 1 - 2 * lax.rem(shard, 2)
    across = lax.rem(shard + 2, 4)
    diagonal = lax.rem(sibling + 2, 4)
    pairs, block, _ = tc.shape
    width = tc.shape[2] // CHUNKS
    rows = width // LANES
    groups = coeff_ref.shape[1]

    barrier = pltpu.get_barrier_semaphore()

    def greet(d, carry):
        pl.semaphore_signal(
            barrier, inc=1, device_id={"mu": lax.rem(me + d + 1, n)}, device_id_type=MESH
        )
        return carry

    loop(n - 1, greet, 0)
    for peer in (sibling, across, diagonal):
        pl.semaphore_signal(barrier, inc=1, device_id={"pa": peer}, device_id_type=MESH)

    def tc_copy(c):
        columns = pl.ds(c * width, width)
        return pltpu.make_async_copy(
            tc_hbm.at[:, :, columns], tc.at[:, :, columns], tc_sem.at[c]
        )

    small = [
        pltpu.make_async_copy(source, target, small_sem.at[i])
        for i, (source, target) in enumerate((
            (mu_hbm, mu_ref), (site_hbm, site_ref), (pos_hbm, pos_ref), (coeff_hbm, coeff_ref),
        ))
    ]
    for copy in small:
        copy.start()
    for c in range(CHUNKS):
        tc_copy(c).start()
    site = lax.rem(me, SITES)
    fit_copy = pltpu.make_async_copy(
        fit_hbm.at[pl.ds(site * NU_SITE, NU_SITE)], fit, fit_sem
    )
    fit_copy.start()

    for copy in small:
        copy.wait()
    slots = []
    for t in range(pairs):
        rank = jnp.int32(0)
        for u in range(t):
            rank += (site_ref[0, u] == site_ref[0, t]).astype(jnp.int32)
        slots.append(site_ref[0, t] * CAP + rank)
    key_row = lax.broadcasted_iota(jnp.int32, (SLOTS, LANES), 0)
    table = jnp.full((SLOTS, LANES), -1.0, F32)
    for t in range(pairs):
        table = jnp.where(key_row == slots[t], pos_ref[0, t].astype(F32), table)
    first_half = lax.broadcasted_iota(jnp.int32, (1, LANES), 1) < block
    for s in range(SITES):
        keys_out[s] = jnp.where(
            first_half, table[s * CAP:s * CAP + 1, :], table[s * CAP + 1:s * CAP + 2, :]
        )
    keys_in[0] = keys_out[site]
    slot_row = lax.broadcasted_iota(jnp.int32, (groups, SLOTS, LANES), 1).reshape(
        groups * SLOTS, LANES
    )
    lane = lax.broadcasted_iota(jnp.int32, (groups * SLOTS, LANES), 1)
    halves = []
    for t in range(pairs):
        mu = mu_ref[0, t]
        two = coeff_ref[lax.shift_right_logical(mu, 1)].astype(F32)
        wide = jnp.broadcast_to(two[:, None, :], (groups, SLOTS, LANES))
        wide = wide.reshape(groups * SLOTS, LANES)
        moved = lax.bitwise_and(mu + t, 1) == 1
        wide = jnp.where(moved, pltpu.roll(wide, block, 1), wide)
        halves.append(jnp.where(slot_row == slots[t], wide, 0.0))
    left = []
    for t in range(0, pairs, 2):
        if t + 1 < pairs:
            left.append(jnp.where(lane < block, halves[t], halves[t + 1]).astype(BF16))
        else:
            left.append(halves[t][:, :block].astype(BF16))

    def key_copy(d):
        return pltpu.make_async_remote_copy(
            src_ref=keys_out.at[lax.rem(lax.rem(me + d, n), SITES)], dst_ref=keys_in.at[d],
            send_sem=key_send.at[d], recv_sem=key_recv.at[d],
            device_id={"mu": lax.rem(me + d, n)}, device_id_type=MESH,
        )

    def pay_copy(c, d):
        owner = lax.rem(me + d, n)
        return pltpu.make_async_remote_copy(
            src_ref=payload.at[c, owner], dst_ref=arrived.at[c, d],
            send_sem=pay_send.at[c, d], recv_sem=pay_recv.at[c, d],
            device_id={"mu": owner}, device_id_type=MESH,
        )

    def make_payload(c):
        tc_copy(c).wait()
        for j in range(0, rows, 2):
            start = c * width + j * LANES
            acc = None
            for t, part in zip(range(0, pairs, 2), left):
                depth = part.shape[1]
                right = tc[t:t + depth // block, :, start:start + 2 * LANES]
                term = jnp.dot(
                    part, right.reshape(depth, 2 * LANES), preferred_element_type=F32
                )
                acc = term if acc is None else acc + term
            turned[pl.ds(j, n * CAP, stride=rows), :] = acc[:, :LANES]
            turned[pl.ds(j + 1, n * CAP, stride=rows), :] = acc[:, LANES:]

        def pack(w, carry):
            first = w * CAP * rows
            if not isinstance(w, int):
                first = pl.multiple_of(first, CAP * rows)
            payload[c, w] = turned[pl.ds(first, CAP * rows), :].astype(BF16)
            return carry

        loop(n, pack, 0)
        arrived[c, 0] = payload[c, me]

    order = list(range(1, n))
    if n <= 16:
        order.sort(key=lambda d: abs(d - n // 2))

    def each_peer(act):
        if n <= 16:
            for d in order:
                act(d)
        else:
            def body(d, carry):
                act(d)
                return carry
            lax.fori_loop(1, n, body, 0)

    for c in range(CHUNKS):
        make_payload(c)
        if c == 0:
            pl.semaphore_wait(barrier, n - 1 + 3)
            each_peer(lambda d: key_copy(d).start())
        each_peer(lambda d, c=c: pay_copy(c, d).start())

    each_peer(lambda d: key_copy(d).wait_recv())

    def pa_copy(c, which, target, send, recv):
        return pltpu.make_async_remote_copy(
            src_ref=gath.at[c, which], dst_ref=gath.at[c, which],
            send_sem=send.at[c], recv_sem=recv.at[c],
            device_id={"pa": target}, device_id_type=MESH,
        )

    def x_copy(c):
        return pa_copy(c, shard, across, x_send, x_recv)

    def sib_copy(c):
        return pa_copy(c, shard, sibling, sib_send, sib_recv)

    def fwd_copy(c):
        return pa_copy(c, across, sibling, fwd_send, fwd_recv)

    for c in range(CHUNKS):
        def add_source(d, sums, c=c):
            sums = list(sums)
            both = keys_in[d]
            other = pltpu.roll(both, block, 1)
            for cap in range(CAP):
                key = jnp.where(first_half, *((both, other) if cap == 0 else (other, both)))
                value = arrived[c, d, cap * rows:(cap + 1) * rows, :].astype(F32)
                for k in range(NU_SITE):
                    sums[k] = sums[k] + jnp.where(key == float(k), value, 0.0)
            return tuple(sums)

        sums = tuple(jnp.zeros((rows, LANES), F32) for _ in range(NU_SITE))
        if n <= 16:
            sums = add_source(0, sums)
            for d in reversed(order):
                pay_copy(c, d).wait_recv()
                sums = add_source(d, sums)
        else:
            each_peer(lambda d, c=c: pay_copy(c, d).wait_recv())
            sums = lax.fori_loop(0, n, add_source, sums)
        for k in range(NU_SITE):
            gath[c, shard, k * rows:(k + 1) * rows, :] = sums[k].astype(BF16)
        x_copy(c).start()
        sib_copy(c).start()

    def lines(k, which):
        return jnp.concatenate(
            [gath[c, which, k * rows:(k + 1) * rows, :] for c in range(CHUNKS)], axis=0
        )

    fit_copy.wait()
    half_lane = lax.broadcasted_iota(jnp.int32, (CHUNKS * rows, LANES), 1) < block

    def product(k, chip):
        low, high = lines(k, 2 * chip), lines(k, 2 * chip + 1)
        even = jnp.where(half_lane, low, pltpu.roll(high, block, 1))
        odd = jnp.where(half_lane, pltpu.roll(low, block, 1), high)
        held = fit[k, :, pl.ds(pl.multiple_of(chip * LANES, LANES), LANES)]
        both = lax.dot_general(
            jnp.concatenate([even, odd], axis=0), jnp.concatenate([held, held], axis=0),
            (((1,), (1,)), ((), ())), preferred_element_type=F32,
        )
        return jnp.where(half_lane, both[:CHUNKS * rows], both[CHUNKS * rows:])

    chip = lax.div(shard, 2)
    for c in range(CHUNKS):
        sib_copy(c).wait_recv()
    for k in range(NU_SITE):
        total[k] = product(k, chip)
    for c in range(CHUNKS):
        x_copy(c).wait_recv()
        fwd_copy(c).start()
    for c in range(CHUNKS):
        fwd_copy(c).wait_recv()
    for k in range(NU_SITE):
        spread[pl.ds(k, CHUNKS * rows, stride=16), :] = total[k] + product(k, 1 - chip)
    for j in range(CHUNKS * rows):
        out_ref[:, j * LANES:(j + 1) * LANES] = spread[j * 16:j * 16 + NU_SITE, :].astype(BF16)

    each_peer(lambda d: key_copy(d).wait_send())
    for c in range(CHUNKS):
        each_peer(lambda d, c=c: pay_copy(c, d).wait_send())
        x_copy(c).wait_send()
        sib_copy(c).wait_send()
        fwd_copy(c).wait_send()


def local(three_center, pair_mu, pair_site, pair_pos, coeff, fitting):
    n = lax.axis_size("mu")
    pairs, block, columns = three_center.shape
    orbitals = coeff.shape[1]
    shards = lax.axis_size("pa")
    rows = columns // CHUNKS // LANES
    pair_blocks = coeff.reshape(coeff.shape[0] // LANES, LANES, orbitals).transpose(0, 2, 1)
    vmem = pl.BlockSpec(memory_space=pltpu.VMEM)
    hbm = pl.BlockSpec(memory_space=pltpu.HBM)
    dma = pltpu.SemaphoreType.DMA
    result = pl.pallas_call(
        functools.partial(kernel, n),
        out_shape=jax.ShapeDtypeStruct((NU_SITE, columns), BF16),
        in_specs=[hbm] * 6,
        out_specs=vmem,
        scratch_shapes=[
            pltpu.SMEM((1, pairs), jnp.int32),
            pltpu.SMEM((1, pairs), jnp.int32),
            pltpu.SMEM((1, pairs), jnp.int32),
            pltpu.VMEM(pair_blocks.shape, BF16),
            pltpu.VMEM((pairs, block, columns), BF16),
            pltpu.VMEM((NU_SITE,) + fitting.shape[1:], BF16),
            pltpu.VMEM((n * CAP * rows, LANES), F32),
            pltpu.VMEM((CHUNKS, n, CAP * rows, LANES), BF16),
            pltpu.VMEM((CHUNKS, n, CAP * rows, LANES), BF16),
            pltpu.VMEM((SITES, 1, LANES), F32),
            pltpu.VMEM((n, 1, LANES), F32),
            pltpu.VMEM((CHUNKS, shards, NU_SITE * rows, LANES), BF16),
            pltpu.VMEM((NU_SITE, columns // LANES, LANES), F32),
            pltpu.VMEM((columns // LANES * 16, LANES), F32),
            dma((4,)), dma((CHUNKS,)), dma,
            dma((n,)), dma((n,)), dma((CHUNKS, n)), dma((CHUNKS, n)),
            dma((CHUNKS,)), dma((CHUNKS,)), dma((CHUNKS,)),
            dma((CHUNKS,)), dma((CHUNKS,)), dma((CHUNKS,)),
        ],
        compiler_params=pltpu.CompilerParams(
            collective_id=0, has_side_effects=True, vmem_limit_bytes=VMEM_BYTES
        ),
    )(*(
        pltpu.with_memory_space_constraint(operand, pltpu.HBM)
        for operand in (
            pair_mu, pair_site[:, :, 0], pair_pos, pair_blocks, three_center, fitting
        )
    ))
    return result.reshape((1, NU_SITE, 1, columns))


def solution(mesh):
    in_specs = (
        P("mu", None, "pa"),
        P("mu", None),
        P("mu", None, None),
        P("mu", None),
        P(),
        P(None, "pa", None),
    )
    out_specs = P("mu", None, None, "pa")
    return jax.shard_map(local, mesh=mesh, in_specs=in_specs, out_specs=out_specs, check_vma=False)
```

```python
import functools

import jax
import jax.numpy as jnp
from jax import lax
from jax.experimental import pallas as pl
from jax.experimental.pallas import tpu as pltpu
from jax.sharding import PartitionSpec as P

SITES = 4
NU_SITE = 12
CAP = 2
SLOTS = SITES * CAP
LANES = 128
CHUNKS = 4
LAG = 2
VMEM_BYTES = 40 * 1024 * 1024
MESH = pl.DeviceIdType.MESH
F32 = jnp.float32
BF16 = jnp.bfloat16


def loop(count, body, carry):
    if count <= 16:
        for step in range(count):
            carry = body(step, carry)
        return carry
    return lax.fori_loop(0, count, body, carry)


def kernel(
    n, mu_hbm, site_hbm, pos_hbm, coeff_hbm, tc_hbm, fit_hbm, out_ref,
    mu_ref, site_ref, pos_ref, coeff_ref, tc, fit, turned, payload, arrived, keys_out, keys_in, gath, total, spread,
    small_sem, tc_sem, fit_sem, key_send, key_recv, pay_send, pay_recv,
    x_send, x_recv, sib_send, sib_recv, fwd_send, fwd_recv,
):
    me = lax.axis_index("mu")
    shard = lax.axis_index("pa")
    sibling = shard + 1 - 2 * lax.rem(shard, 2)
    across = lax.rem(shard + 2, 4)
    diagonal = lax.rem(sibling + 2, 4)
    pairs, block, _ = tc.shape
    width = tc.shape[2] // CHUNKS
    rows = width // LANES
    groups = coeff_ref.shape[1]

    barrier = pltpu.get_barrier_semaphore()

    def greet(d, carry):
        pl.semaphore_signal(
            barrier, inc=1, device_id={"mu": lax.rem(me + d + 1, n)}, device_id_type=MESH
        )
        return carry

    loop(n - 1, greet, 0)
    for peer in (sibling, across, diagonal):
        pl.semaphore_signal(barrier, inc=1, device_id={"pa": peer}, device_id_type=MESH)

    def tc_copy(c):
        columns = pl.ds(c * width, width)
        return pltpu.make_async_copy(
            tc_hbm.at[:, :, columns], tc.at[:, :, columns], tc_sem.at[c]
        )

    small = [
        pltpu.make_async_copy(source, target, small_sem.at[i])
        for i, (source, target) in enumerate((
            (mu_hbm, mu_ref), (site_hbm, site_ref), (pos_hbm, pos_ref), (coeff_hbm, coeff_ref),
        ))
    ]
    for copy in small:
        copy.start()
    for c in range(CHUNKS):
        tc_copy(c).start()
    site = lax.rem(me, SITES)
    fit_copy = pltpu.make_async_copy(
        fit_hbm.at[pl.ds(site * NU_SITE, NU_SITE)], fit, fit_sem
    )
    fit_copy.start()

    for copy in small:
        copy.wait()
    slots = []
    for t in range(pairs):
        rank = jnp.int32(0)
        for u in range(t):
            rank += (site_ref[0, u] == site_ref[0, t]).astype(jnp.int32)
        slots.append(site_ref[0, t] * CAP + rank)
    key_row = lax.broadcasted_iota(jnp.int32, (SLOTS, LANES), 0)
    table = jnp.full((SLOTS, LANES), -1.0, F32)
    for t in range(pairs):
        table = jnp.where(key_row == slots[t], pos_ref[0, t].astype(F32), table)
    first_half = lax.broadcasted_iota(jnp.int32, (1, LANES), 1) < block
    for s in range(SITES):
        keys_out[s] = jnp.where(
            first_half, table[s * CAP:s * CAP + 1, :], table[s * CAP + 1:s * CAP + 2, :]
        )
    keys_in[0] = keys_out[site]
    slot_row = lax.broadcasted_iota(jnp.int32, (groups, SLOTS, LANES), 1).reshape(
        groups * SLOTS, LANES
    )
    lane = lax.broadcasted_iota(jnp.int32, (groups * SLOTS, LANES), 1)
    halves = []
    for t in range(pairs):
        mu = mu_ref[0, t]
        two = coeff_ref[lax.shift_right_logical(mu, 1)].astype(F32)
        wide = jnp.broadcast_to(two[:, None, :], (groups, SLOTS, LANES))
        wide = wide.reshape(groups * SLOTS, LANES)
        moved = lax.bitwise_and(mu + t, 1) == 1
        wide = jnp.where(moved, pltpu.roll(wide, block, 1), wide)
        halves.append(jnp.where(slot_row == slots[t], wide, 0.0))
    left = []
    for t in range(0, pairs, 2):
        if t + 1 < pairs:
            left.append(jnp.where(lane < block, halves[t], halves[t + 1]).astype(BF16))
        else:
            left.append(halves[t][:, :block].astype(BF16))

    def key_copy(d):
        return pltpu.make_async_remote_copy(
            src_ref=keys_out.at[lax.rem(lax.rem(me + d, n), SITES)], dst_ref=keys_in.at[d],
            send_sem=key_send.at[d], recv_sem=key_recv.at[d],
            device_id={"mu": lax.rem(me + d, n)}, device_id_type=MESH,
        )

    def pay_copy(c, d):
        owner = lax.rem(me + d, n)
        return pltpu.make_async_remote_copy(
            src_ref=payload.at[c, owner], dst_ref=arrived.at[c, d],
            send_sem=pay_send.at[c, d], recv_sem=pay_recv.at[c, d],
            device_id={"mu": owner}, device_id_type=MESH,
        )

    def make_payload(c):
        tc_copy(c).wait()
        for j in range(0, rows, 2):
            start = c * width + j * LANES
            acc = None
            for t, part in zip(range(0, pairs, 2), left):
                depth = part.shape[1]
                right = tc[t:t + depth // block, :, start:start + 2 * LANES]
                term = jnp.dot(
                    part, right.reshape(depth, 2 * LANES), preferred_element_type=F32
                )
                acc = term if acc is None else acc + term
            turned[pl.ds(j, n * CAP, stride=rows), :] = acc[:, :LANES]
            turned[pl.ds(j + 1, n * CAP, stride=rows), :] = acc[:, LANES:]

        def pack(w, carry):
            first = w * CAP * rows
            if not isinstance(w, int):
                first = pl.multiple_of(first, CAP * rows)
            payload[c, w] = turned[pl.ds(first, CAP * rows), :].astype(BF16)
            return carry

        loop(n, pack, 0)
        arrived[c, 0] = payload[c, me]

    order = list(range(1, n))
    if n <= 16:
        order.sort(key=lambda d: abs(d - n // 2))

    def each_peer(act):
        if n <= 16:
            for d in order:
                act(d)
        else:
            def body(d, carry):
                act(d)
                return carry
            lax.fori_loop(1, n, body, 0)

    for c in range(CHUNKS):
        make_payload(c)
        if c == 0:
            pl.semaphore_wait(barrier, n - 1 + 3)
            each_peer(lambda d: key_copy(d).start())
        each_peer(lambda d, c=c: pay_copy(c, d).start())

    each_peer(lambda d: key_copy(d).wait_recv())

    def pa_copy(c, which, target, send, recv):
        return pltpu.make_async_remote_copy(
            src_ref=gath.at[c, which], dst_ref=gath.at[c, which],
            send_sem=send.at[c], recv_sem=recv.at[c],
            device_id={"pa": target}, device_id_type=MESH,
        )

    def x_copy(c):
        return pa_copy(c, shard, across, x_send, x_recv)

    def sib_copy(c):
        return pa_copy(c, shard, sibling, sib_send, sib_recv)

    def fwd_copy(c):
        return pa_copy(c, across, sibling, fwd_send, fwd_recv)

    for c in range(CHUNKS):
        def add_source(d, sums, c=c):
            sums = list(sums)
            both = keys_in[d]
            other = pltpu.roll(both, block, 1)
            for cap in range(CAP):
                key = jnp.where(first_half, *((both, other) if cap == 0 else (other, both)))
                value = arrived[c, d, cap * rows:(cap + 1) * rows, :].astype(F32)
                for k in range(NU_SITE):
                    sums[k] = sums[k] + jnp.where(key == float(k), value, 0.0)
            return tuple(sums)

        sums = tuple(jnp.zeros((rows, LANES), F32) for _ in range(NU_SITE))
        if n <= 16:
            sums = add_source(0, sums)
            for d in reversed(order):
                pay_copy(c, d).wait_recv()
                sums = add_source(d, sums)
        else:
            each_peer(lambda d, c=c: pay_copy(c, d).wait_recv())
            sums = lax.fori_loop(0, n, add_source, sums)
        for k in range(NU_SITE):
            gath[c, shard, k * rows:(k + 1) * rows, :] = sums[k].astype(BF16)
        x_copy(c).start()
        sib_copy(c).start()
        if c >= LAG:
            x_copy(c - LAG).wait_recv()
            fwd_copy(c - LAG).start()

    def lines(k, which):
        return jnp.concatenate(
            [gath[c, which, k * rows:(k + 1) * rows, :] for c in range(CHUNKS)], axis=0
        )

    fit_copy.wait()
    half_lane = lax.broadcasted_iota(jnp.int32, (CHUNKS * rows, LANES), 1) < block

    def product(k, chip):
        low, high = lines(k, 2 * chip), lines(k, 2 * chip + 1)
        even = jnp.where(half_lane, low, pltpu.roll(high, block, 1))
        odd = jnp.where(half_lane, pltpu.roll(low, block, 1), high)
        held = fit[k, :, pl.ds(pl.multiple_of(chip * LANES, LANES), LANES)]
        both = lax.dot_general(
            jnp.concatenate([even, odd], axis=0), jnp.concatenate([held, held], axis=0),
            (((1,), (1,)), ((), ())), preferred_element_type=F32,
        )
        return jnp.where(half_lane, both[:CHUNKS * rows], both[CHUNKS * rows:])

    chip = lax.div(shard, 2)
    for c in range(CHUNKS):
        sib_copy(c).wait_recv()
    for k in range(NU_SITE):
        total[k] = product(k, chip)
    for c in range(CHUNKS - LAG, CHUNKS):
        x_copy(c).wait_recv()
        fwd_copy(c).start()
    for c in range(CHUNKS):
        fwd_copy(c).wait_recv()
    for k in range(NU_SITE):
        spread[pl.ds(k, CHUNKS * rows, stride=16), :] = total[k] + product(k, 1 - chip)
    for j in range(CHUNKS * rows):
        out_ref[:, j * LANES:(j + 1) * LANES] = spread[j * 16:j * 16 + NU_SITE, :].astype(BF16)

    each_peer(lambda d: key_copy(d).wait_send())
    for c in range(CHUNKS):
        each_peer(lambda d, c=c: pay_copy(c, d).wait_send())
        x_copy(c).wait_send()
        sib_copy(c).wait_send()
        fwd_copy(c).wait_send()


def local(three_center, pair_mu, pair_site, pair_pos, coeff, fitting):
    n = lax.axis_size("mu")
    pairs, block, columns = three_center.shape
    orbitals = coeff.shape[1]
    shards = lax.axis_size("pa")
    rows = columns // CHUNKS // LANES
    pair_blocks = coeff.reshape(coeff.shape[0] // LANES, LANES, orbitals).transpose(0, 2, 1)
    vmem = pl.BlockSpec(memory_space=pltpu.VMEM)
    hbm = pl.BlockSpec(memory_space=pltpu.HBM)
    dma = pltpu.SemaphoreType.DMA
    result = pl.pallas_call(
        functools.partial(kernel, n),
        out_shape=jax.ShapeDtypeStruct((NU_SITE, columns), BF16),
        in_specs=[hbm] * 6,
        out_specs=vmem,
        scratch_shapes=[
            pltpu.SMEM((1, pairs), jnp.int32),
            pltpu.SMEM((1, pairs), jnp.int32),
            pltpu.SMEM((1, pairs), jnp.int32),
            pltpu.VMEM(pair_blocks.shape, BF16),
            pltpu.VMEM((pairs, block, columns), BF16),
            pltpu.VMEM((NU_SITE,) + fitting.shape[1:], BF16),
            pltpu.VMEM((n * CAP * rows, LANES), F32),
            pltpu.VMEM((CHUNKS, n, CAP * rows, LANES), BF16),
            pltpu.VMEM((CHUNKS, n, CAP * rows, LANES), BF16),
            pltpu.VMEM((SITES, 1, LANES), F32),
            pltpu.VMEM((n, 1, LANES), F32),
            pltpu.VMEM((CHUNKS, shards, NU_SITE * rows, LANES), BF16),
            pltpu.VMEM((NU_SITE, columns // LANES, LANES), F32),
            pltpu.VMEM((columns // LANES * 16, LANES), F32),
            dma((4,)), dma((CHUNKS,)), dma,
            dma((n,)), dma((n,)), dma((CHUNKS, n)), dma((CHUNKS, n)),
            dma((CHUNKS,)), dma((CHUNKS,)), dma((CHUNKS,)),
            dma((CHUNKS,)), dma((CHUNKS,)), dma((CHUNKS,)),
        ],
        compiler_params=pltpu.CompilerParams(
            collective_id=0, has_side_effects=True, vmem_limit_bytes=VMEM_BYTES
        ),
    )(*(
        pltpu.with_memory_space_constraint(operand, pltpu.HBM)
        for operand in (
            pair_mu, pair_site[:, :, 0], pair_pos, pair_blocks, three_center, fitting
        )
    ))
    return result.reshape((1, NU_SITE, 1, columns))


def solution(mesh):
    in_specs = (
        P("mu", None, "pa"),
        P("mu", None),
        P("mu", None, None),
        P("mu", None),
        P(),
        P(None, "pa", None),
    )
    out_specs = P("mu", None, None, "pa")
    return jax.shard_map(local, mesh=mesh, in_specs=in_specs, out_specs=out_specs, check_vma=False)
```

```python
import functools

import jax
import jax.numpy as jnp
from jax import lax
from jax.experimental import pallas as pl
from jax.experimental.pallas import tpu as pltpu
from jax.sharding import PartitionSpec as P

SITES = 4
NU_SITE = 12
CAP = 2
SLOTS = SITES * CAP
LANES = 128
CHUNKS = 2
PARTS = 2
HELD = NU_SITE // PARTS
VMEM_BYTES = 40 * 1024 * 1024
MESH = pl.DeviceIdType.MESH
F32 = jnp.float32
BF16 = jnp.bfloat16


def loop(count, body, carry):
    if count <= 16:
        for step in range(count):
            carry = body(step, carry)
        return carry
    return lax.fori_loop(0, count, body, carry)


def kernel(
    n, mu_hbm, site_hbm, pos_hbm, coeff_hbm, tc_hbm, fit_hbm, out_ref,
    mu_ref, site_ref, pos_ref, coeff_ref, tc, fit, turned, payload, arrived, keys_out, keys_in, gath, total, spread,
    small_sem, tc_sem, fit_sem, key_send, key_recv, pay_send, pay_recv,
    x_send, x_recv, sib_send, sib_recv, fwd_send, fwd_recv,
):
    me = lax.axis_index("mu")
    shard = lax.axis_index("pa")
    sibling = shard + 1 - 2 * lax.rem(shard, 2)
    across = lax.rem(shard + 2, 4)
    diagonal = lax.rem(sibling + 2, 4)
    pairs, block, _ = tc.shape
    width = tc.shape[2] // CHUNKS
    rows = tc.shape[2] // LANES
    groups = coeff_ref.shape[1]

    barrier = pltpu.get_barrier_semaphore()

    def greet(d, carry):
        pl.semaphore_signal(
            barrier, inc=1, device_id={"mu": lax.rem(me + d + 1, n)}, device_id_type=MESH
        )
        return carry

    loop(n - 1, greet, 0)
    for peer in (sibling, across, diagonal):
        pl.semaphore_signal(barrier, inc=1, device_id={"pa": peer}, device_id_type=MESH)

    def tc_copy(c):
        columns = pl.ds(c * width, width)
        return pltpu.make_async_copy(
            tc_hbm.at[:, :, columns], tc.at[:, :, columns], tc_sem.at[c]
        )

    small = [
        pltpu.make_async_copy(source, target, small_sem.at[i])
        for i, (source, target) in enumerate((
            (mu_hbm, mu_ref), (site_hbm, site_ref), (pos_hbm, pos_ref), (coeff_hbm, coeff_ref),
        ))
    ]
    for copy in small:
        copy.start()
    for c in range(CHUNKS):
        tc_copy(c).start()
    site = lax.rem(me, SITES)
    fit_copy = pltpu.make_async_copy(
        fit_hbm.at[pl.ds(site * NU_SITE, NU_SITE)], fit, fit_sem
    )
    fit_copy.start()

    for copy in small:
        copy.wait()
    slots = []
    for t in range(pairs):
        rank = jnp.int32(0)
        for u in range(t):
            rank += (site_ref[0, u] == site_ref[0, t]).astype(jnp.int32)
        slots.append(site_ref[0, t] * CAP + rank)
    key_row = lax.broadcasted_iota(jnp.int32, (SLOTS, LANES), 0)
    table = jnp.full((SLOTS, LANES), -1.0, F32)
    for t in range(pairs):
        table = jnp.where(key_row == slots[t], pos_ref[0, t].astype(F32), table)
    first_half = lax.broadcasted_iota(jnp.int32, (1, LANES), 1) < block
    for s in range(SITES):
        keys_out[s] = jnp.where(
            first_half, table[s * CAP:s * CAP + 1, :], table[s * CAP + 1:s * CAP + 2, :]
        )
    keys_in[0] = keys_out[site]
    slot_row = lax.broadcasted_iota(jnp.int32, (groups, SLOTS, LANES), 1).reshape(
        groups * SLOTS, LANES
    )
    lane = lax.broadcasted_iota(jnp.int32, (groups * SLOTS, LANES), 1)
    halves = []
    for t in range(pairs):
        mu = mu_ref[0, t]
        two = coeff_ref[lax.shift_right_logical(mu, 1)].astype(F32)
        wide = jnp.broadcast_to(two[:, None, :], (groups, SLOTS, LANES))
        wide = wide.reshape(groups * SLOTS, LANES)
        moved = lax.bitwise_and(mu + t, 1) == 1
        wide = jnp.where(moved, pltpu.roll(wide, block, 1), wide)
        halves.append(jnp.where(slot_row == slots[t], wide, 0.0))
    left = []
    for t in range(0, pairs, 2):
        if t + 1 < pairs:
            left.append(jnp.where(lane < block, halves[t], halves[t + 1]).astype(BF16))
        else:
            left.append(halves[t][:, :block].astype(BF16))

    def key_copy(d):
        return pltpu.make_async_remote_copy(
            src_ref=keys_out.at[lax.rem(lax.rem(me + d, n), SITES)], dst_ref=keys_in.at[d],
            send_sem=key_send.at[d], recv_sem=key_recv.at[d],
            device_id={"mu": lax.rem(me + d, n)}, device_id_type=MESH,
        )

    def pay_copy(d):
        owner = lax.rem(me + d, n)
        return pltpu.make_async_remote_copy(
            src_ref=payload.at[owner], dst_ref=arrived.at[d],
            send_sem=pay_send.at[d], recv_sem=pay_recv.at[d],
            device_id={"mu": owner}, device_id_type=MESH,
        )

    def transform(c):
        tc_copy(c).wait()
        for j in range(c * width // LANES, (c + 1) * width // LANES, 2):
            start = j * LANES
            acc = None
            for t, part in zip(range(0, pairs, 2), left):
                depth = part.shape[1]
                right = tc[t:t + depth // block, :, start:start + 2 * LANES]
                term = jnp.dot(
                    part, right.reshape(depth, 2 * LANES), preferred_element_type=F32
                )
                acc = term if acc is None else acc + term
            turned[pl.ds(j, n * CAP, stride=rows), :] = acc[:, :LANES]
            turned[pl.ds(j + 1, n * CAP, stride=rows), :] = acc[:, LANES:]

    order = list(range(1, n))
    if n <= 16:
        order.sort(key=lambda d: abs(d - n // 2))

    def each_peer(act):
        if n <= 16:
            for d in order:
                act(d)
        else:
            def body(d, carry):
                act(d)
                return carry
            lax.fori_loop(1, n, body, 0)

    pl.semaphore_wait(barrier, n - 1 + 3)
    each_peer(lambda d: key_copy(d).start())
    for c in range(CHUNKS):
        transform(c)

    def pack(w, carry):
        first = w * CAP * rows
        if not isinstance(w, int):
            first = pl.multiple_of(first, CAP * rows)
        payload[w] = turned[pl.ds(first, CAP * rows), :].astype(BF16)
        return carry

    loop(n, pack, 0)
    each_peer(lambda d: pay_copy(d).start())
    arrived[0] = payload[me]

    each_peer(lambda d: key_copy(d).wait_recv())

    def pa_copy(c, which, target, send, recv):
        return pltpu.make_async_remote_copy(
            src_ref=gath.at[c, which], dst_ref=gath.at[c, which],
            send_sem=send.at[c], recv_sem=recv.at[c],
            device_id={"pa": target}, device_id_type=MESH,
        )

    def x_copy(c):
        return pa_copy(c, shard, across, x_send, x_recv)

    def sib_copy(c):
        return pa_copy(c, shard, sibling, sib_send, sib_recv)

    def fwd_copy(c):
        return pa_copy(c, across, sibling, fwd_send, fwd_recv)

    for c in range(PARTS):
        def add_source(d, sums, c=c):
            sums = list(sums)
            both = keys_in[d]
            other = pltpu.roll(both, block, 1)
            for cap in range(CAP):
                key = jnp.where(first_half, *((both, other) if cap == 0 else (other, both)))
                value = arrived[d, cap * rows:(cap + 1) * rows, :].astype(F32)
                for k in range(HELD):
                    sums[k] = sums[k] + jnp.where(key == float(c * HELD + k), value, 0.0)
            return tuple(sums)

        sums = tuple(jnp.zeros((rows, LANES), F32) for _ in range(HELD))
        if n <= 16:
            sums = add_source(0, sums)
            for d in reversed(order):
                if c == 0:
                    pay_copy(d).wait_recv()
                sums = add_source(d, sums)
        else:
            if c == 0:
                each_peer(lambda d: pay_copy(d).wait_recv())
            sums = lax.fori_loop(0, n, add_source, sums)
        for k in range(HELD):
            gath[c, shard, k * rows:(k + 1) * rows, :] = sums[k].astype(BF16)
        x_copy(c).start()
        sib_copy(c).start()

    fit_copy.wait()
    half_lane = lax.broadcasted_iota(jnp.int32, (rows, LANES), 1) < block

    def product(c, k, chip):
        low = gath[c, 2 * chip, k * rows:(k + 1) * rows, :]
        high = gath[c, 2 * chip + 1, k * rows:(k + 1) * rows, :]
        even = jnp.where(half_lane, low, pltpu.roll(high, block, 1))
        odd = jnp.where(half_lane, pltpu.roll(low, block, 1), high)
        held = fit[c * HELD + k, :, pl.ds(pl.multiple_of(chip * LANES, LANES), LANES)]
        both = lax.dot_general(
            jnp.concatenate([even, odd], axis=0), jnp.concatenate([held, held], axis=0),
            (((1,), (1,)), ((), ())), preferred_element_type=F32,
        )
        return jnp.where(half_lane, both[:rows], both[rows:])

    chip = lax.div(shard, 2)
    for c in range(PARTS):
        sib_copy(c).wait_recv()
        for k in range(HELD):
            total[c * HELD + k] = product(c, k, chip)
    for c in range(PARTS):
        x_copy(c).wait_recv()
        fwd_copy(c).start()
    for c in range(PARTS):
        fwd_copy(c).wait_recv()
        for k in range(HELD):
            at = c * HELD + k
            spread[pl.ds(at, rows, stride=16), :] = total[at] + product(c, k, 1 - chip)
    for j in range(rows):
        out_ref[:, j * LANES:(j + 1) * LANES] = spread[j * 16:j * 16 + NU_SITE, :].astype(BF16)

    each_peer(lambda d: key_copy(d).wait_send())
    each_peer(lambda d: pay_copy(d).wait_send())
    for c in range(PARTS):
        x_copy(c).wait_send()
        sib_copy(c).wait_send()
        fwd_copy(c).wait_send()


def local(three_center, pair_mu, pair_site, pair_pos, coeff, fitting):
    n = lax.axis_size("mu")
    pairs, block, columns = three_center.shape
    orbitals = coeff.shape[1]
    shards = lax.axis_size("pa")
    rows = columns // LANES
    pair_blocks = coeff.reshape(coeff.shape[0] // LANES, LANES, orbitals).transpose(0, 2, 1)
    vmem = pl.BlockSpec(memory_space=pltpu.VMEM)
    hbm = pl.BlockSpec(memory_space=pltpu.HBM)
    dma = pltpu.SemaphoreType.DMA
    result = pl.pallas_call(
        functools.partial(kernel, n),
        out_shape=jax.ShapeDtypeStruct((NU_SITE, columns), BF16),
        in_specs=[hbm] * 6,
        out_specs=vmem,
        scratch_shapes=[
            pltpu.SMEM((1, pairs), jnp.int32),
            pltpu.SMEM((1, pairs), jnp.int32),
            pltpu.SMEM((1, pairs), jnp.int32),
            pltpu.VMEM(pair_blocks.shape, BF16),
            pltpu.VMEM((pairs, block, columns), BF16),
            pltpu.VMEM((NU_SITE,) + fitting.shape[1:], BF16),
            pltpu.VMEM((n * CAP * rows, LANES), F32),
            pltpu.VMEM((n, CAP * rows, LANES), BF16),
            pltpu.VMEM((n, CAP * rows, LANES), BF16),
            pltpu.VMEM((SITES, 1, LANES), F32),
            pltpu.VMEM((n, 1, LANES), F32),
            pltpu.VMEM((PARTS, shards, HELD * rows, LANES), BF16),
            pltpu.VMEM((NU_SITE, columns // LANES, LANES), F32),
            pltpu.VMEM((columns // LANES * 16, LANES), F32),
            dma((4,)), dma((CHUNKS,)), dma,
            dma((n,)), dma((n,)), dma((n,)), dma((n,)),
            dma((PARTS,)), dma((PARTS,)), dma((PARTS,)),
            dma((PARTS,)), dma((PARTS,)), dma((PARTS,)),
        ],
        compiler_params=pltpu.CompilerParams(
            collective_id=0, has_side_effects=True, vmem_limit_bytes=VMEM_BYTES
        ),
    )(*(
        pltpu.with_memory_space_constraint(operand, pltpu.HBM)
        for operand in (
            pair_mu, pair_site[:, :, 0], pair_pos, pair_blocks, three_center, fitting
        )
    ))
    return result.reshape((1, NU_SITE, 1, columns))


def solution(mesh):
    in_specs = (
        P("mu", None, "pa"),
        P("mu", None),
        P("mu", None, None),
        P("mu", None),
        P(),
        P(None, "pa", None),
    )
    out_specs = P("mu", None, None, "pa")
    return jax.shard_map(local, mesh=mesh, in_specs=in_specs, out_specs=out_specs, check_vma=False)
```

```python
import functools

import jax
import jax.numpy as jnp
from jax import lax
from jax.experimental import pallas as pl
from jax.experimental.pallas import tpu as pltpu
from jax.sharding import PartitionSpec as P

SITES = 4
NU_SITE = 12
CAP = 2
SLOTS = SITES * CAP
LANES = 128
CHUNKS = 2
VMEM_BYTES = 40 * 1024 * 1024
MESH = pl.DeviceIdType.MESH
F32 = jnp.float32
BF16 = jnp.bfloat16


def loop(count, body, carry):
    if count <= 16:
        for step in range(count):
            carry = body(step, carry)
        return carry
    return lax.fori_loop(0, count, body, carry)


def kernel(
    n, mu_hbm, site_hbm, pos_hbm, coeff_hbm, tc_hbm, fit_hbm, out_ref,
    mu_ref, site_ref, pos_ref, coeff_ref, tc, fit, turned, payload, arrived, keys_out, keys_in, gath, weights, total, spread,
    small_sem, tc_sem, fit_sem, key_send, key_recv, pay_send, pay_recv,
    x_send, x_recv, sib_send, sib_recv, fwd_send, fwd_recv,
):
    me = lax.axis_index("mu")
    shard = lax.axis_index("pa")
    sibling = shard + 1 - 2 * lax.rem(shard, 2)
    across = lax.rem(shard + 2, 4)
    diagonal = lax.rem(sibling + 2, 4)
    pairs, block, _ = tc.shape
    width = tc.shape[2] // CHUNKS
    rows = width // LANES
    groups = coeff_ref.shape[1]

    barrier = pltpu.get_barrier_semaphore()

    def greet(d, carry):
        pl.semaphore_signal(
            barrier, inc=1, device_id={"mu": lax.rem(me + d + 1, n)}, device_id_type=MESH
        )
        return carry

    loop(n - 1, greet, 0)
    for peer in (sibling, across, diagonal):
        pl.semaphore_signal(barrier, inc=1, device_id={"pa": peer}, device_id_type=MESH)

    def tc_copy(c):
        columns = pl.ds(c * width, width)
        return pltpu.make_async_copy(
            tc_hbm.at[:, :, columns], tc.at[:, :, columns], tc_sem.at[c]
        )

    small = [
        pltpu.make_async_copy(source, target, small_sem.at[i])
        for i, (source, target) in enumerate((
            (mu_hbm, mu_ref), (site_hbm, site_ref), (pos_hbm, pos_ref), (coeff_hbm, coeff_ref),
        ))
    ]
    for copy in small:
        copy.start()
    for c in range(CHUNKS):
        tc_copy(c).start()
    site = lax.rem(me, SITES)
    fit_copy = pltpu.make_async_copy(
        fit_hbm.at[pl.ds(site * NU_SITE, NU_SITE)], fit, fit_sem
    )
    fit_copy.start()

    for copy in small:
        copy.wait()
    slots = []
    for t in range(pairs):
        rank = jnp.int32(0)
        for u in range(t):
            rank += (site_ref[0, u] == site_ref[0, t]).astype(jnp.int32)
        slots.append(site_ref[0, t] * CAP + rank)
    key_row = lax.broadcasted_iota(jnp.int32, (SLOTS, LANES), 0)
    table = jnp.full((SLOTS, LANES), -1.0, F32)
    for t in range(pairs):
        table = jnp.where(key_row == slots[t], pos_ref[0, t].astype(F32), table)
    first_half = lax.broadcasted_iota(jnp.int32, (1, LANES), 1) < block
    for s in range(SITES):
        keys_out[s] = jnp.where(
            first_half, table[s * CAP:s * CAP + 1, :], table[s * CAP + 1:s * CAP + 2, :]
        )
    keys_in[0] = keys_out[site]
    slot_row = lax.broadcasted_iota(jnp.int32, (groups, SLOTS, LANES), 1).reshape(
        groups * SLOTS, LANES
    )
    lane = lax.broadcasted_iota(jnp.int32, (groups * SLOTS, LANES), 1)
    halves = []
    for t in range(pairs):
        mu = mu_ref[0, t]
        two = coeff_ref[lax.shift_right_logical(mu, 1)].astype(F32)
        wide = jnp.broadcast_to(two[:, None, :], (groups, SLOTS, LANES))
        wide = wide.reshape(groups * SLOTS, LANES)
        moved = lax.bitwise_and(mu + t, 1) == 1
        wide = jnp.where(moved, pltpu.roll(wide, block, 1), wide)
        halves.append(jnp.where(slot_row == slots[t], wide, 0.0))
    left = []
    for t in range(0, pairs, 2):
        if t + 1 < pairs:
            left.append(jnp.where(lane < block, halves[t], halves[t + 1]).astype(BF16))
        else:
            left.append(halves[t][:, :block].astype(BF16))

    def key_copy(d):
        return pltpu.make_async_remote_copy(
            src_ref=keys_out.at[lax.rem(lax.rem(me + d, n), SITES)], dst_ref=keys_in.at[d],
            send_sem=key_send.at[d], recv_sem=key_recv.at[d],
            device_id={"mu": lax.rem(me + d, n)}, device_id_type=MESH,
        )

    def pay_copy(c, d):
        owner = lax.rem(me + d, n)
        return pltpu.make_async_remote_copy(
            src_ref=payload.at[c, owner], dst_ref=arrived.at[c, d],
            send_sem=pay_send.at[c, d], recv_sem=pay_recv.at[c, d],
            device_id={"mu": owner}, device_id_type=MESH,
        )

    def make_payload(c):
        tc_copy(c).wait()
        for j in range(0, rows, 2):
            start = c * width + j * LANES
            acc = None
            for t, part in zip(range(0, pairs, 2), left):
                depth = part.shape[1]
                right = tc[t:t + depth // block, :, start:start + 2 * LANES]
                term = jnp.dot(
                    part, right.reshape(depth, 2 * LANES), preferred_element_type=F32
                )
                acc = term if acc is None else acc + term
            turned[pl.ds(j, n * CAP, stride=rows), :] = acc[:, :LANES]
            turned[pl.ds(j + 1, n * CAP, stride=rows), :] = acc[:, LANES:]

        def pack(w, carry):
            first = w * CAP * rows
            if not isinstance(w, int):
                first = pl.multiple_of(first, CAP * rows)
            payload[c, w] = turned[pl.ds(first, CAP * rows), :].astype(BF16)
            return carry

        loop(n, pack, 0)
        arrived[c, 0] = payload[c, me]

    order = list(range(1, n))
    if n <= 16:
        order.sort(key=lambda d: abs(d - n // 2))

    def each_peer(act):
        if n <= 16:
            for d in order:
                act(d)
        else:
            def body(d, carry):
                act(d)
                return carry
            lax.fori_loop(1, n, body, 0)

    pl.semaphore_wait(barrier, n - 1 + 3)
    each_peer(lambda d: key_copy(d).start())
    for c in range(CHUNKS):
        make_payload(c)
        each_peer(lambda d, c=c: pay_copy(c, d).start())

    fit_copy.wait()
    for k in range(NU_SITE):
        double = jnp.concatenate([fit[k], fit[k]], axis=0)
        flipped = double.T
        lane_w = lax.broadcasted_iota(jnp.int32, (block, 2 * block), 1)
        for q in range(4):
            piece = flipped[q * block:(q + 1) * block, :]
            zero = jnp.zeros_like(piece)
            weights[k, q, 0:block, :] = jnp.where(lane_w < block, piece, zero)
            weights[k, q, block:2 * block, :] = jnp.where(lane_w < block, zero, piece)

    each_peer(lambda d: key_copy(d).wait_recv())

    def pa_copy(c, which, target, send, recv):
        return pltpu.make_async_remote_copy(
            src_ref=gath.at[c, which], dst_ref=gath.at[c, which],
            send_sem=send.at[c], recv_sem=recv.at[c],
            device_id={"pa": target}, device_id_type=MESH,
        )

    def x_copy(c):
        return pa_copy(c, shard, across, x_send, x_recv)

    def sib_copy(c):
        return pa_copy(c, shard, sibling, sib_send, sib_recv)

    def fwd_copy(c):
        return pa_copy(c, across, sibling, fwd_send, fwd_recv)

    for c in range(CHUNKS):
        def add_source(d, sums, c=c):
            sums = list(sums)
            both = keys_in[d]
            other = pltpu.roll(both, block, 1)
            for cap in range(CAP):
                key = jnp.where(first_half, *((both, other) if cap == 0 else (other, both)))
                value = arrived[c, d, cap * rows:(cap + 1) * rows, :].astype(F32)
                for k in range(NU_SITE):
                    sums[k] = sums[k] + jnp.where(key == float(k), value, 0.0)
            return tuple(sums)

        sums = tuple(jnp.zeros((rows, LANES), F32) for _ in range(NU_SITE))
        if n <= 16:
            sums = add_source(0, sums)
            for d in reversed(order):
                pay_copy(c, d).wait_recv()
                sums = add_source(d, sums)
        else:
            each_peer(lambda d, c=c: pay_copy(c, d).wait_recv())
            sums = lax.fori_loop(0, n, add_source, sums)
        for k in range(NU_SITE):
            gath[c, shard, k * rows:(k + 1) * rows, :] = sums[k].astype(BF16)
        x_copy(c).start()
        sib_copy(c).start()

    def lines(k, which):
        return jnp.concatenate(
            [gath[c, which, k * rows:(k + 1) * rows, :] for c in range(CHUNKS)], axis=0
        )

    def product(k, which):
        return jnp.dot(lines(k, which), weights[k, which], preferred_element_type=F32)

    for c in range(CHUNKS):
        sib_copy(c).wait_recv()
    first = 2 * lax.div(shard, 2)
    for k in range(NU_SITE):
        pair = jnp.concatenate([lines(k, first), lines(k, first + 1)], axis=1)
        held = weights[k, pl.ds(first, 2)].reshape(4 * block, LANES)
        total[k] = jnp.dot(pair, held, preferred_element_type=F32)
    for c in range(CHUNKS):
        x_copy(c).wait_recv()
        fwd_copy(c).start()
    for k in range(NU_SITE):
        total[k] += product(k, across)
    for c in range(CHUNKS):
        fwd_copy(c).wait_recv()
    for k in range(NU_SITE):
        spread[pl.ds(k, CHUNKS * rows, stride=16), :] = total[k] + product(k, diagonal)
    for j in range(CHUNKS * rows):
        out_ref[:, j * LANES:(j + 1) * LANES] = spread[j * 16:j * 16 + NU_SITE, :].astype(BF16)

    each_peer(lambda d: key_copy(d).wait_send())
    for c in range(CHUNKS):
        each_peer(lambda d, c=c: pay_copy(c, d).wait_send())
        x_copy(c).wait_send()
        sib_copy(c).wait_send()
        fwd_copy(c).wait_send()


def local(three_center, pair_mu, pair_site, pair_pos, coeff, fitting):
    n = lax.axis_size("mu")
    pairs, block, columns = three_center.shape
    orbitals = coeff.shape[1]
    shards = lax.axis_size("pa")
    rows = columns // CHUNKS // LANES
    pair_blocks = coeff.reshape(coeff.shape[0] // LANES, LANES, orbitals).transpose(0, 2, 1)
    vmem = pl.BlockSpec(memory_space=pltpu.VMEM)
    hbm = pl.BlockSpec(memory_space=pltpu.HBM)
    dma = pltpu.SemaphoreType.DMA
    result = pl.pallas_call(
        functools.partial(kernel, n),
        out_shape=jax.ShapeDtypeStruct((NU_SITE, columns), BF16),
        in_specs=[hbm] * 6,
        out_specs=vmem,
        scratch_shapes=[
            pltpu.SMEM((1, pairs), jnp.int32),
            pltpu.SMEM((1, pairs), jnp.int32),
            pltpu.SMEM((1, pairs), jnp.int32),
            pltpu.VMEM(pair_blocks.shape, BF16),
            pltpu.VMEM((pairs, block, columns), BF16),
            pltpu.VMEM((NU_SITE,) + fitting.shape[1:], BF16),
            pltpu.VMEM((n * CAP * rows, LANES), F32),
            pltpu.VMEM((CHUNKS, n, CAP * rows, LANES), BF16),
            pltpu.VMEM((CHUNKS, n, CAP * rows, LANES), BF16),
            pltpu.VMEM((SITES, 1, LANES), F32),
            pltpu.VMEM((n, 1, LANES), F32),
            pltpu.VMEM((CHUNKS, shards, NU_SITE * rows, LANES), BF16),
            pltpu.VMEM((NU_SITE, shards, 2 * block, LANES), BF16),
            pltpu.VMEM((NU_SITE, columns // LANES, LANES), F32),
            pltpu.VMEM((columns // LANES * 16, LANES), F32),
            dma((4,)), dma((CHUNKS,)), dma,
            dma((n,)), dma((n,)), dma((CHUNKS, n)), dma((CHUNKS, n)),
            dma((CHUNKS,)), dma((CHUNKS,)), dma((CHUNKS,)),
            dma((CHUNKS,)), dma((CHUNKS,)), dma((CHUNKS,)),
        ],
        compiler_params=pltpu.CompilerParams(
            collective_id=0, has_side_effects=True, vmem_limit_bytes=VMEM_BYTES
        ),
    )(*(
        pltpu.with_memory_space_constraint(operand, pltpu.HBM)
        for operand in (
            pair_mu, pair_site[:, :, 0], pair_pos, pair_blocks, three_center, fitting
        )
    ))
    return result.reshape((1, NU_SITE, 1, columns))


def solution(mesh):
    in_specs = (
        P("mu", None, "pa"),
        P("mu", None),
        P("mu", None, None),
        P("mu", None),
        P(),
        P(None, "pa", None),
    )
    out_specs = P("mu", None, None, "pa")
    return jax.shard_map(local, mesh=mesh, in_specs=in_specs, out_specs=out_specs, check_vma=False)
```

```python
import functools

import jax
import jax.numpy as jnp
from jax import lax
from jax.experimental import pallas as pl
from jax.experimental.pallas import tpu as pltpu
from jax.sharding import PartitionSpec as P

SITES = 4
NU_SITE = 12
CAP = 2
SLOTS = SITES * CAP
LANES = 128
CHUNKS = 2
VMEM_BYTES = 40 * 1024 * 1024
MESH = pl.DeviceIdType.MESH
F32 = jnp.float32
BF16 = jnp.bfloat16


def loop(count, body, carry):
    if count <= 16:
        for step in range(count):
            carry = body(step, carry)
        return carry
    return lax.fori_loop(0, count, body, carry)


def kernel(
    n, mu_hbm, site_hbm, pos_hbm, coeff_hbm, tc_hbm, fit_hbm, out_ref,
    mu_ref, site_ref, pos_ref, coeff_ref, tc, fit, turned, payload, arrived, keys_out, keys_in, gath, weights, total, spread,
    small_sem, tc_sem, fit_sem, key_send, key_recv, pay_send, pay_recv,
    x_send, x_recv, sib_send, sib_recv, fwd_send, fwd_recv,
):
    me = lax.axis_index("mu")
    shard = lax.axis_index("pa")
    sibling = shard + 1 - 2 * lax.rem(shard, 2)
    across = lax.rem(shard + 2, 4)
    diagonal = lax.rem(sibling + 2, 4)
    pairs, block, _ = tc.shape
    width = tc.shape[2] // CHUNKS
    rows = width // LANES
    groups = coeff_ref.shape[1]

    def tc_copy(c):
        columns = pl.ds(c * width, width)
        return pltpu.make_async_copy(
            tc_hbm.at[:, :, columns], tc.at[:, :, columns], tc_sem.at[c]
        )

    small = [
        pltpu.make_async_copy(source, target, small_sem.at[i])
        for i, (source, target) in enumerate((
            (mu_hbm, mu_ref), (site_hbm, site_ref), (pos_hbm, pos_ref), (coeff_hbm, coeff_ref),
        ))
    ]
    for copy in small:
        copy.start()
    for c in range(CHUNKS):
        tc_copy(c).start()
    site = lax.rem(me, SITES)
    fit_copy = pltpu.make_async_copy(
        fit_hbm.at[pl.ds(site * NU_SITE, NU_SITE)], fit, fit_sem
    )
    fit_copy.start()

    barrier = pltpu.get_barrier_semaphore()

    def greet(d, carry):
        pl.semaphore_signal(
            barrier, inc=1, device_id={"mu": lax.rem(me + d + 1, n)}, device_id_type=MESH
        )
        return carry

    loop(n - 1, greet, 0)
    for peer in (sibling, across, diagonal):
        pl.semaphore_signal(barrier, inc=1, device_id={"pa": peer}, device_id_type=MESH)

    for copy in small:
        copy.wait()
    slots = []
    for t in range(pairs):
        rank = jnp.int32(0)
        for u in range(t):
            rank += (site_ref[0, u] == site_ref[0, t]).astype(jnp.int32)
        slots.append(site_ref[0, t] * CAP + rank)
    key_row = lax.broadcasted_iota(jnp.int32, (SLOTS, LANES), 0)
    table = jnp.full((SLOTS, LANES), -1.0, F32)
    for t in range(pairs):
        table = jnp.where(key_row == slots[t], pos_ref[0, t].astype(F32), table)
    first_half = lax.broadcasted_iota(jnp.int32, (1, LANES), 1) < block
    for s in range(SITES):
        keys_out[s] = jnp.where(
            first_half, table[s * CAP:s * CAP + 1, :], table[s * CAP + 1:s * CAP + 2, :]
        )
    keys_in[0] = keys_out[site]
    slot_row = lax.broadcasted_iota(jnp.int32, (groups, SLOTS, LANES), 1).reshape(
        groups * SLOTS, LANES
    )
    lane = lax.broadcasted_iota(jnp.int32, (groups * SLOTS, LANES), 1)
    halves = []
    for t in range(pairs):
        mu = mu_ref[0, t]
        two = coeff_ref[lax.shift_right_logical(mu, 1)].astype(F32)
        wide = jnp.broadcast_to(two[:, None, :], (groups, SLOTS, LANES))
        wide = wide.reshape(groups * SLOTS, LANES)
        moved = lax.bitwise_and(mu + t, 1) == 1
        wide = jnp.where(moved, pltpu.roll(wide, block, 1), wide)
        halves.append(jnp.where(slot_row == slots[t], wide, 0.0))
    left = []
    for t in range(0, pairs, 2):
        if t + 1 < pairs:
            left.append(jnp.where(lane < block, halves[t], halves[t + 1]).astype(BF16))
        else:
            left.append(halves[t][:, :block].astype(BF16))

    def key_copy(d):
        return pltpu.make_async_remote_copy(
            src_ref=keys_out.at[lax.rem(lax.rem(me + d, n), SITES)], dst_ref=keys_in.at[d],
            send_sem=key_send.at[d], recv_sem=key_recv.at[d],
            device_id={"mu": lax.rem(me + d, n)}, device_id_type=MESH,
        )

    def pay_copy(c, d):
        owner = lax.rem(me + d, n)
        return pltpu.make_async_remote_copy(
            src_ref=payload.at[c, owner], dst_ref=arrived.at[c, d],
            send_sem=pay_send.at[c, d], recv_sem=pay_recv.at[c, d],
            device_id={"mu": owner}, device_id_type=MESH,
        )

    def make_payload(c):
        tc_copy(c).wait()
        for j in range(0, rows, 2):
            start = c * width + j * LANES
            acc = None
            for t, part in zip(range(0, pairs, 2), left):
                depth = part.shape[1]
                right = tc[t:t + depth // block, :, start:start + 2 * LANES]
                term = jnp.dot(
                    part, right.reshape(depth, 2 * LANES), preferred_element_type=F32
                )
                acc = term if acc is None else acc + term
            turned[pl.ds(j, n * CAP, stride=rows), :] = acc[:, :LANES]
            turned[pl.ds(j + 1, n * CAP, stride=rows), :] = acc[:, LANES:]

        def pack(w, carry):
            first = w * CAP * rows
            if not isinstance(w, int):
                first = pl.multiple_of(first, CAP * rows)
            payload[c, w] = turned[pl.ds(first, CAP * rows), :].astype(BF16)
            return carry

        loop(n, pack, 0)
        arrived[c, 0] = payload[c, me]

    order = list(range(1, n))
    if n <= 16:
        order.sort(key=lambda d: abs(d - n // 2))

    def each_peer(act):
        if n <= 16:
            for d in order:
                act(d)
        else:
            def body(d, carry):
                act(d)
                return carry
            lax.fori_loop(1, n, body, 0)

    for c in range(CHUNKS):
        make_payload(c)
        if c == 0:
            pl.semaphore_wait(barrier, n - 1 + 3)
            each_peer(lambda d: key_copy(d).start())
        each_peer(lambda d, c=c: pay_copy(c, d).start())

    fit_copy.wait()
    for k in range(NU_SITE):
        double = jnp.concatenate([fit[k], fit[k]], axis=0)
        flipped = double.T
        lane_w = lax.broadcasted_iota(jnp.int32, (block, 2 * block), 1)
        for q in range(4):
            piece = flipped[q * block:(q + 1) * block, :]
            zero = jnp.zeros_like(piece)
            weights[k, q, 0:block, :] = jnp.where(lane_w < block, piece, zero)
            weights[k, q, block:2 * block, :] = jnp.where(lane_w < block, zero, piece)

    each_peer(lambda d: key_copy(d).wait_recv())

    def pa_copy(c, which, target, send, recv):
        return pltpu.make_async_remote_copy(
            src_ref=gath.at[c, which], dst_ref=gath.at[c, which],
            send_sem=send.at[c], recv_sem=recv.at[c],
            device_id={"pa": target}, device_id_type=MESH,
        )

    def x_copy(c):
        return pa_copy(c, shard, across, x_send, x_recv)

    def sib_copy(c):
        return pa_copy(c, shard, sibling, sib_send, sib_recv)

    def fwd_copy(c):
        return pa_copy(c, across, sibling, fwd_send, fwd_recv)

    for c in range(CHUNKS):
        def add_source(d, sums, c=c):
            sums = list(sums)
            both = keys_in[d]
            other = pltpu.roll(both, block, 1)
            for cap in range(CAP):
                key = jnp.where(first_half, *((both, other) if cap == 0 else (other, both)))
                value = arrived[c, d, cap * rows:(cap + 1) * rows, :].astype(F32)
                for k in range(NU_SITE):
                    sums[k] = sums[k] + jnp.where(key == float(k), value, 0.0)
            return tuple(sums)

        sums = tuple(jnp.zeros((rows, LANES), F32) for _ in range(NU_SITE))
        if n <= 16:
            sums = add_source(0, sums)
            for d in reversed(order):
                pay_copy(c, d).wait_recv()
                sums = add_source(d, sums)
        else:
            each_peer(lambda d, c=c: pay_copy(c, d).wait_recv())
            sums = lax.fori_loop(0, n, add_source, sums)
        for k in range(NU_SITE):
            gath[c, shard, k * rows:(k + 1) * rows, :] = sums[k].astype(BF16)
        x_copy(c).start()
        sib_copy(c).start()

    def lines(k, which):
        return jnp.concatenate(
            [gath[c, which, k * rows:(k + 1) * rows, :] for c in range(CHUNKS)], axis=0
        )

    def product(k, which):
        return jnp.dot(lines(k, which), weights[k, which], preferred_element_type=F32)

    for c in range(CHUNKS):
        sib_copy(c).wait_recv()
    x_copy(0).wait_recv()
    fwd_copy(0).start()
    first = 2 * lax.div(shard, 2)
    for k in range(NU_SITE):
        pair = jnp.concatenate([lines(k, first), lines(k, first + 1)], axis=1)
        held = weights[k, pl.ds(first, 2)].reshape(4 * block, LANES)
        total[k] = jnp.dot(pair, held, preferred_element_type=F32)
    for c in range(1, CHUNKS):
        x_copy(c).wait_recv()
        fwd_copy(c).start()
    for k in range(NU_SITE):
        total[k] += product(k, across)
    for c in range(CHUNKS):
        fwd_copy(c).wait_recv()
    for k in range(NU_SITE):
        spread[pl.ds(k, CHUNKS * rows, stride=16), :] = total[k] + product(k, diagonal)
    for j in range(CHUNKS * rows):
        out_ref[:, j * LANES:(j + 1) * LANES] = spread[j * 16:j * 16 + NU_SITE, :].astype(BF16)

    each_peer(lambda d: key_copy(d).wait_send())
    for c in range(CHUNKS):
        each_peer(lambda d, c=c: pay_copy(c, d).wait_send())
        x_copy(c).wait_send()
        sib_copy(c).wait_send()
        fwd_copy(c).wait_send()


def local(three_center, pair_mu, pair_site, pair_pos, coeff, fitting):
    n = lax.axis_size("mu")
    pairs, block, columns = three_center.shape
    orbitals = coeff.shape[1]
    shards = lax.axis_size("pa")
    rows = columns // CHUNKS // LANES
    pair_blocks = coeff.reshape(coeff.shape[0] // LANES, LANES, orbitals).transpose(0, 2, 1)
    vmem = pl.BlockSpec(memory_space=pltpu.VMEM)
    hbm = pl.BlockSpec(memory_space=pltpu.HBM)
    dma = pltpu.SemaphoreType.DMA
    result = pl.pallas_call(
        functools.partial(kernel, n),
        out_shape=jax.ShapeDtypeStruct((NU_SITE, columns), BF16),
        in_specs=[hbm] * 6,
        out_specs=vmem,
        scratch_shapes=[
            pltpu.SMEM((1, pairs), jnp.int32),
            pltpu.SMEM((1, pairs), jnp.int32),
            pltpu.SMEM((1, pairs), jnp.int32),
            pltpu.VMEM(pair_blocks.shape, BF16),
            pltpu.VMEM((pairs, block, columns), BF16),
            pltpu.VMEM((NU_SITE,) + fitting.shape[1:], BF16),
            pltpu.VMEM((n * CAP * rows, LANES), F32),
            pltpu.VMEM((CHUNKS, n, CAP * rows, LANES), BF16),
            pltpu.VMEM((CHUNKS, n, CAP * rows, LANES), BF16),
            pltpu.VMEM((SITES, 1, LANES), F32),
            pltpu.VMEM((n, 1, LANES), F32),
            pltpu.VMEM((CHUNKS, shards, NU_SITE * rows, LANES), BF16),
            pltpu.VMEM((NU_SITE, shards, 2 * block, LANES), BF16),
            pltpu.VMEM((NU_SITE, columns // LANES, LANES), F32),
            pltpu.VMEM((columns // LANES * 16, LANES), F32),
            dma((4,)), dma((CHUNKS,)), dma,
            dma((n,)), dma((n,)), dma((CHUNKS, n)), dma((CHUNKS, n)),
            dma((CHUNKS,)), dma((CHUNKS,)), dma((CHUNKS,)),
            dma((CHUNKS,)), dma((CHUNKS,)), dma((CHUNKS,)),
        ],
        compiler_params=pltpu.CompilerParams(
            collective_id=0, has_side_effects=True, vmem_limit_bytes=VMEM_BYTES
        ),
    )(*(
        pltpu.with_memory_space_constraint(operand, pltpu.HBM)
        for operand in (
            pair_mu, pair_site[:, :, 0], pair_pos, pair_blocks, three_center, fitting
        )
    ))
    return result.reshape((1, NU_SITE, 1, columns))


def solution(mesh):
    in_specs = (
        P("mu", None, "pa"),
        P("mu", None),
        P("mu", None, None),
        P("mu", None),
        P(),
        P(None, "pa", None),
    )
    out_specs = P("mu", None, None, "pa")
    return jax.shard_map(local, mesh=mesh, in_specs=in_specs, out_specs=out_specs, check_vma=False)
```
